32 devices in a mesh: item: 8 (over y, x, core), week: 4 (over z).
Axes of the slice: x: 2, y: 2, z: 4, core: 2. Of those that a mesh axis runs over, the one named last changes fastest.
Arguments:
- counts: int32 [128, 256, 16384], P(None, 'week', 'item'), may hold values from 0 to 7, as said below
- user_factor: float32 [128, 64], replicated, may hold values from 0.3 to 1.5
- item_factor: float32 [16384, 64], P('item'), may hold values from 0.001 to 12, as said below
- week_factor: float32 [256, 64], P('week'), may hold values from 0.001 to 1.5, as said below
Outputs:
- updated_users: float32 [128, 64], replicated
The draws below stay inside these ranges and needn't reach their ends.
Inputs may be any that keep to these rules, and one draw needn't show every extreme that they name: `counts`: every user has at least one positive count. `item_factor`: positive entries. `week_factor`: positive entries.
All inputs are finite; a program needn't handle non-finite values.
Results may differ from the reference program's by a relative error of at most 0.0003.
Values sent between devices are 32-bit elements; how exact they have to be, the bound alone decides.
No kernel may reach another device: no remote copies, remote signals or barrier semaphores. Data moves between devices by JAX's collectives and lax.ppermute only.
A program may use at most 320 MiB of HBM per device.

```python
import math
import jax
import jax.numpy as jnp
from jax import lax

USERS = 128
ITEMS = 16384
WEEKS = 256
RANK = 64
ITERS = 3


def item_groups(key):
    group_key = jax.random.fold_in(key, 5)
    return jax.random.randint(group_key, (ITEMS,), 0, RANK)


def positive_field(key, length, field_scale):
    base = jnp.exp(jax.random.uniform(key, (length, RANK), jnp.float32, math.log(0.3), math.log(3.0)))
    rise = 2.0
    position = jnp.arange(length, dtype=jnp.float32)[:, None] / max(length - 1, 1)
    return field_scale * base * (1.0 + rise * position)


def draw_item_factor(key, part):
    groups = item_groups(key)
    key = jax.random.fold_in(key, 11)
    base = positive_field(key, ITEMS, 0.04)
    column_index = jnp.arange(RANK, dtype=jnp.int32)[None, :]
    favoured = (groups[:, None] == column_index).astype(jnp.float32)
    return base * (1.0 + 20.0 * favoured)


def draw_week_factor(key, part):
    key = jax.random.fold_in(key, 23)
    return positive_field(key, WEEKS, 0.05)


def draw_counts(key, part):
    groups = item_groups(key)
    key = jax.random.fold_in(key, 37)
    taste_key, weekly_key, anchor_key, moment_key = jax.random.split(key, 4)
    liked = jax.random.randint(taste_key, (USERS, RANK), 0, 2)
    liked_items = liked[:, groups]
    anchor = jax.random.randint(anchor_key, (USERS, 1, 1), 0, ITEMS)
    week_anchor = jax.random.randint(moment_key, (USERS, 1, 1), 0, WEEKS)
    item_index = jnp.arange(ITEMS, dtype=jnp.int32)[None, None, :]
    week_index = jnp.arange(WEEKS, dtype=jnp.int32)[None, :, None]
    strong = jnp.maximum(jax.random.randint(weekly_key, (USERS, WEEKS, ITEMS), 0, 17) - 9, 0)
    faint = jnp.where(strong == 7, 1, 0)
    result = jnp.where(liked_items[:, None, :] == 1, strong, faint)
    result = jnp.where((item_index == anchor) & (week_index == week_anchor), 7, result)
    return result.astype(jnp.int32)


def setup_inputs(seed: int = 0) -> dict:
    streams_of = jax.random.split(jax.random.key(seed), 5)
    counts = draw_counts(jax.random.fold_in(streams_of[4], 71), 0)
    user_factor = jnp.clip(jnp.exp(jax.random.uniform(streams_of[1], (USERS, RANK), jnp.float32, math.log(0.3), math.log(1.5))), 0.3, 1.5)
    item_factor = draw_item_factor(jax.random.fold_in(streams_of[4], 71), 0)
    week_factor = draw_week_factor(jax.random.fold_in(streams_of[4], 71), 0)
    return {"counts": counts, "user_factor": user_factor, "item_factor": item_factor, "week_factor": week_factor}


def block_phi(factor, counts, item_factor, week_factor):
    item_block = min(256, ITEMS)
    blocks = ITEMS // item_block

    def accumulate(total, index):
        start = (index * item_block).astype(jnp.int32)
        block_counts = lax.dynamic_slice_in_dim(counts, start, item_block, 2)
        block_items = lax.dynamic_slice_in_dim(item_factor, start, item_block, 0)
        khatri_rao = (week_factor[:, None, :] * block_items[None, :, :]).reshape(-1, RANK)
        model = jnp.dot(factor, khatri_rao.T, precision=lax.Precision.HIGHEST)
        ratio = block_counts.reshape(USERS, -1).astype(jnp.float32) / model
        return total + jnp.dot(ratio, khatri_rao, precision=lax.Precision.HIGHEST), None

    start_total = jnp.zeros((USERS, RANK), jnp.float32)
    total, unused = lax.scan(accumulate, start_total, jnp.arange(blocks, dtype=jnp.int32))
    return total


def reference(counts, user_factor, item_factor, week_factor):
    denominator = jnp.sum(item_factor, axis=0) * jnp.sum(week_factor, axis=0)
    factor = user_factor
    for iteration in range(ITERS):
        phi = block_phi(factor, counts, item_factor, week_factor)
        factor = factor * phi / denominator[None, :]
    return factor
```

```python
import functools

import jax
import jax.numpy as jnp
from jax import lax
from jax.experimental import pallas as pl
from jax.experimental.pallas import tpu as pltpu
from jax.sharding import PartitionSpec as P

ITERS = 3
CHUNKS = 2
BLOCK_USERS = 8
COLUMNS = 256
AXES = ("item", "week")
F32, BF16 = jnp.float32, jnp.bfloat16


def split(x):
    high = x.astype(BF16)
    low = (x - high.astype(F32)).astype(BF16)
    return high, low


def pack(x):
    half = x.shape[0] // 2
    return jnp.concatenate([x[:half], x[half:]], axis=1)


def unpack(x):
    rank = x.shape[1] // 2
    return jnp.concatenate([x[:, :rank], x[:, rank:]], axis=0)


def prepare(item_t, model_w, phi_w):
    high, low = split(item_t)
    model_w[...] = jnp.concatenate([high, high, low, low], axis=0)
    phi_w[...] = jnp.concatenate([high.astype(F32), low.astype(F32)], axis=0).T.astype(BF16)


def column_sums(phi_w, week, n_item, n_week):
    rank = week.shape[1]
    ones = jnp.ones((8, phi_w.shape[0]), BF16)
    both = jnp.dot(ones, phi_w[...], preferred_element_type=F32)
    items = (both[:, :rank] + both[:, rank:]) * (1.0 / n_week)
    weeks = jnp.broadcast_to(jnp.sum(week, axis=0, keepdims=True), items.shape) * (1.0 / n_item)
    return jnp.concatenate([items, weeks], axis=1)


def phi_block(counts, factor, week, model_w, phi_w):
    users, weeks, items = counts.shape
    rank = factor.shape[1]
    rows = users * weeks
    scaled = (factor[:, None, :] * week[None, :, :]).reshape(rows, rank)
    high, low = split(scaled)
    lhs = jnp.concatenate([high, low, high, low], axis=1)
    total = None
    for start in range(0, items, COLUMNS):
        at = slice(start, start + COLUMNS)
        model = jnp.dot(lhs, model_w[:, at], preferred_element_type=F32)
        count = counts[:, :, at].reshape(rows, COLUMNS).astype(F32)
        ratio = count * pltpu.reciprocal(model, approx=True)
        rhs = phi_w[at, :]
        part = jnp.dot(
            jnp.concatenate(split(ratio), axis=1),
            jnp.concatenate([rhs, rhs], axis=0),
            preferred_element_type=F32,
        )
        total = part if total is None else total + part
    total = (total[:, :rank] + total[:, rank:]).reshape(users, weeks, rank)
    return jnp.sum(total * week[None, :, :], axis=1)


def step(counts, week, model_w, phi_w, factor_s, phi_s):
    i = pl.program_id(0)
    block = pl.ds(pl.multiple_of(i * BLOCK_USERS, BLOCK_USERS), BLOCK_USERS)
    phi_s[block, :] = phi_block(counts, factor_s[block, :], week[...], model_w, phi_w)


def first_kernel(chunk, n_item, n_week, prep, *refs):
    if prep:
        counts, factor_t, week, item_t, out, model_w, phi_w, factor_s, phi_s = refs
    else:
        counts, factor_t, week, model_w, phi_w, out, factor_s, phi_s = refs
    users = phi_s.shape[0]

    @pl.when(pl.program_id(0) == 0)
    def _():
        if prep:
            prepare(item_t[...], model_w, phi_w)
        factor_s[...] = factor_t[...].T[chunk * users:(chunk + 1) * users, :]

    step(counts, week, model_w, phi_w, factor_s, phi_s)

    @pl.when(pl.program_id(0) == pl.num_programs(0) - 1)
    def _():
        out[: users // 2, :] = pack(phi_s[...])
        out[users // 2:, :] = column_sums(phi_w, week[...], n_item, n_week)


def denominators(sums):
    rank = sums.shape[1] // 2
    return sums[:, :rank] * sums[:, rank:]


def second_kernel(chunk, counts, factor_t, gathered, week, model_w, phi_w, out, factor_s, den, phi_s):
    users = phi_s.shape[0]

    @pl.when(pl.program_id(0) == 0)
    def _():
        summed = jnp.sum(gathered[...], axis=0)
        den[...] = denominators(summed[users // 2:])
        old = factor_t[...].T[chunk * users:(chunk + 1) * users, :]
        factor_s[...] = old * unpack(summed[: users // 2]) / den[0:1, :]

    step(counts, week, model_w, phi_w, factor_s, phi_s)

    @pl.when(pl.program_id(0) == pl.num_programs(0) - 1)
    def _():
        out[...] = pack(phi_s[...])


def third_kernel(counts, factor, gathered, den, week, model_w, phi_w, out, factor_s, phi_s):
    @pl.when(pl.program_id(0) == 0)
    def _():
        summed = jnp.sum(gathered[...], axis=0)
        factor_s[...] = factor[...] * unpack(summed) / den[0:1, :]

    step(counts, week, model_w, phi_w, factor_s, phi_s)

    @pl.when(pl.program_id(0) == pl.num_programs(0) - 1)
    def _():
        out[...] = pack(phi_s[...])


def last_kernel(*refs):
    out = refs[-1]
    parts = []
    for factor, gathered, den in zip(refs[0:-1:3], refs[1:-1:3], refs[2:-1:3]):
        summed = jnp.sum(gathered[...], axis=0)
        parts.append(factor[...] * unpack(summed) / den[0:1, :])
    out[...] = jnp.concatenate(parts, axis=0).T


def whole(x):
    shape = x.shape
    return pl.BlockSpec(shape, lambda i: (0,) * len(shape))


def per_device(n_item, n_week, counts, user_factor, item_factor, week_factor):
    all_users, rank = user_factor.shape
    weeks, items = counts.shape[1:]
    users = all_users // CHUNKS
    factor_t, item_t = user_factor.T, item_factor.T

    def shape(dims, dtype=F32):
        return jax.ShapeDtypeStruct(dims, dtype)

    def run(kernel, chunk, operands, outs, scratch):
        steps = users // BLOCK_USERS
        return pl.pallas_call(
            kernel,
            grid=(steps,),
            in_specs=[pl.BlockSpec((BLOCK_USERS, weeks, items), lambda i: (chunk * steps + i, 0, 0))]
            + [whole(x) for x in operands],
            out_specs=[whole(x) for x in outs],
            out_shape=outs,
            scratch_shapes=[pltpu.VMEM((users, rank), F32) for _ in range(scratch)],
            compiler_params=pltpu.CompilerParams(vmem_limit_bytes=40 * 1024 * 1024),
            cost_estimate=pl.CostEstimate(
                flops=2 * 3 * users * weeks * items * 256,
                bytes_accessed=4 * users * weeks * items,
                transcendentals=0,
            ),
        )(counts, *operands)

    def gather(x):
        return lax.all_gather(x, AXES)

    packed = shape((users // 2, 2 * rank))
    packed_sums = shape((users // 2 + 8, 2 * rank))
    weights = [shape((4 * rank, items), BF16), shape((items, 2 * rank), BF16)]

    arrived, factors, dens = [], [], []
    model_w = phi_w = None
    for chunk in range(CHUNKS):
        kernel = functools.partial(first_kernel, chunk, n_item, n_week, chunk == 0)
        if chunk == 0:
            out, model_w, phi_w = run(
                kernel, chunk, (factor_t, week_factor, item_t), [packed_sums] + weights, 2
            )
        else:
            (out,) = run(kernel, chunk, (factor_t, week_factor, model_w, phi_w), [packed_sums], 2)
        arrived.append(gather(out))
    for chunk in range(CHUNKS):
        kernel = functools.partial(second_kernel, chunk)
        out, factor, den = run(
            kernel, chunk, (factor_t, arrived[chunk], week_factor, model_w, phi_w),
            [packed, shape((users, rank)), shape((8, rank))], 1,
        )
        factors.append(factor)
        dens.append(den)
        arrived[chunk] = gather(out)
    for chunk in range(CHUNKS):
        out, factors[chunk] = run(
            third_kernel, chunk,
            (factors[chunk], arrived[chunk], dens[chunk], week_factor, model_w, phi_w),
            [packed, shape((users, rank))], 1,
        )
        arrived[chunk] = gather(out)
    final = pl.pallas_call(last_kernel, out_shape=shape((rank, all_users)))(
        *[x for group in zip(factors, arrived, dens) for x in group]
    )
    return final.T


def solution(mesh):
    sizes = dict(zip(mesh.axis_names, mesh.devices.shape))
    placed = (P(None, "week", "item"), P(), P("item", None), P("week", None))
    run = functools.partial(per_device, sizes["item"], sizes["week"])
    return jax.shard_map(run, mesh=mesh, in_specs=placed, out_specs=P(), check_vma=False)
```

```python
import functools

import jax
import jax.numpy as jnp
from jax import lax
from jax.experimental import pallas as pl
from jax.experimental.pallas import tpu as pltpu
from jax.sharding import PartitionSpec as P

ITERS = 3
PAIRS = 2
TILE_USERS = 8
FIRST_BLOCK, NEXT_BLOCK = 8, 16
COLUMNS = 256
STAGE = 4
F32, BF16 = jnp.float32, jnp.bfloat16


def split(x):
    high = x.astype(BF16)
    low = (x - high.astype(F32)).astype(BF16)
    return high, low


def tree(parts):
    while len(parts) > 1:
        parts = [a + b for a, b in zip(parts[0::2], parts[1::2])]
    return parts[0]


def exchange(x, axis, size, low, width):
    parts = [x]
    for k in range(1, width):
        parts.append(lax.ppermute(x, axis, [(i, i ^ (k * low)) for i in range(size)]))
    return parts


def stages(axes):
    plan = []
    for axis, size in axes:
        if size & (size - 1):
            raise ValueError("axis size")
        while size > 1:
            width = min(STAGE, size)
            size //= width
            plan.append((axis, size, width))
    return plan


def prepare(item_t, model_w, phi_w):
    high, low = split(item_t)
    model_w[...] = jnp.concatenate([high, high, low, low], axis=0)
    phi_w[...] = jnp.concatenate([high.astype(F32), low.astype(F32)], axis=0).T.astype(BF16)


def column_sums(phi_w, week, n_item, n_week):
    rank = week.shape[1]
    ones = jnp.ones((8, phi_w.shape[0]), BF16)
    both = jnp.dot(ones, phi_w[...], preferred_element_type=F32)
    items = (both[:, :rank] + both[:, rank:]) * (1.0 / n_week)
    weeks = jnp.broadcast_to(jnp.sum(week, axis=0, keepdims=True), items.shape) * (1.0 / n_item)
    return jnp.concatenate([items, weeks], axis=1)


def phi_block(counts, factor, week, model_w, phi_w):
    users, weeks, items = counts.shape
    rank = factor.shape[1]
    rows = TILE_USERS * weeks

    def operand(tile):
        mine = factor[tile * TILE_USERS:(tile + 1) * TILE_USERS]
        high, low = split((mine[:, None, :] * week[None, :, :]).reshape(rows, rank))
        return jnp.concatenate([high, low, high, low], axis=1)

    tiles = users // TILE_USERS
    lhs = [operand(tile) for tile in range(tiles)]
    work = [(t, slice(c, c + COLUMNS)) for t in range(tiles) for c in range(0, items, COLUMNS)]

    def model_of(tile, at):
        return jnp.dot(lhs[tile], model_w[:, at], preferred_element_type=F32)

    totals = [None] * tiles
    ahead = model_of(*work[0])
    for n, (tile, at) in enumerate(work):
        model = ahead
        if n + 1 < len(work):
            ahead = model_of(*work[n + 1])
        count = counts[tile * TILE_USERS:(tile + 1) * TILE_USERS, :, at]
        count = count.astype(jnp.int32).astype(F32).reshape(rows, COLUMNS)
        ratio = count * pltpu.reciprocal(model, approx=True)
        rhs = phi_w[at, :]
        part = jnp.dot(
            jnp.concatenate(split(ratio), axis=1),
            jnp.concatenate([rhs, rhs], axis=0),
            preferred_element_type=F32,
        )
        totals[tile] = part if totals[tile] is None else totals[tile] + part
    sums = []
    for total in totals:
        total = (total[:, :rank] + total[:, rank:]).reshape(TILE_USERS, weeks, rank)
        sums.append(jnp.sum(total * week[None, :, :], axis=1))
    return jnp.concatenate(sums, axis=0)


def update_kernel(iteration, half, group, prep, n_item, n_week, n_arrived, names, *refs):
    r = dict(zip(names, refs))
    users, rank = r["factor_s"].shape
    arrived = [r["arrived%d" % k] for k in range(n_arrived)]

    @pl.when(pl.program_id(0) == 0)
    def _():
        if prep:
            prepare(r["item_t"][...], r["model_w"], r["phi_w"])
        if iteration == 0:
            r["factor_s"][...] = r["factor_t"][...].T[group * users:(group + 1) * users, :]
        else:
            summed = tree([a[...] for a in arrived])
            if iteration == 1:
                sums = summed[users:]
                den = sums[:, :rank] * sums[:, rank:]
                r["den_out"][...] = den
                old = r["factor_t"][...].T[group * users:(group + 1) * users, :]
            else:
                den = r["den"][...]
                old = r["factor"][...]
            phi = summed[:users, half * rank:(half + 1) * rank]
            new = old * phi / den[0:1, :]
            r["factor_s"][...] = new
            r["factor_out"][...] = new

    counts = r["counts"]
    block_users = counts.shape[0]
    block = pl.ds(pl.multiple_of(pl.program_id(0) * block_users, block_users), block_users)
    if iteration == 0:
        r["small_out"][...] = counts[...].astype(jnp.int8)
    r["phi_s"][block, :] = phi_block(
        counts, r["factor_s"][block, :], r["week"][...], r["model_w"], r["phi_w"]
    )

    @pl.when(pl.program_id(0) == pl.num_programs(0) - 1)
    def _():
        phi = r["phi_s"][...]
        if half == 0:
            r["phi_out"][...] = phi
        else:
            r["phi_out"][:users, :] = jnp.concatenate([r["partner"][...], phi], axis=1)
            if iteration == 0:
                r["phi_out"][users:, :] = column_sums(r["phi_w"], r["week"][...], n_item, n_week)


def last_kernel(n_arrived, *refs):
    den, out = refs[0], refs[-1]
    rank = den.shape[1]
    rest = refs[1:-1]
    parts = []
    for pair in range(PAIRS):
        mine, rest = rest[: n_arrived + 2], rest[n_arrived + 2:]
        summed = tree([a[...] for a in mine[2:]])
        for half in range(2):
            phi = summed[:, half * rank:(half + 1) * rank]
            parts.append(mine[half][...] * phi / den[0:1, :])
    out[...] = jnp.concatenate(parts, axis=0).T


def whole(x):
    shape = x.shape
    return pl.BlockSpec(shape, lambda i: (0,) * len(shape))


def per_device(axes, counts, user_factor, item_factor, week_factor):
    all_users, rank = user_factor.shape
    weeks, items = counts.shape[1:]
    users = all_users // (2 * PAIRS)
    factor_t, item_t = user_factor.T, item_factor.T
    sizes = dict(axes)
    plan = [
        (axis, sizes[axis], low, width)
        for axis, low, width in stages([("week", sizes["week"]), ("item", sizes["item"])])
    ]
    n_arrived = plan[-1][3]

    def shape(dims, dtype=F32):
        return jax.ShapeDtypeStruct(dims, dtype)

    def run(iteration, half, group, ins, outs, after):
        first = iteration == 0
        block_users = FIRST_BLOCK if first else NEXT_BLOCK
        steps = users // block_users
        block = (block_users, weeks, items)
        offset = group * steps if first else 0
        prep = "model_w" not in dict(ins)
        in_specs = [pl.BlockSpec(block, lambda i: (offset + i, 0, 0))]
        in_specs += [whole(x) for _, x in ins[1:]]
        in_specs += [pl.BlockSpec(memory_space=pl.ANY)] * len(after)
        names = [n for n, _ in ins] + ["after%d" % k for k in range(len(after))]
        out_specs = [
            pl.BlockSpec(block, lambda i: (i, 0, 0)) if n == "small_out" else whole(s)
            for n, s in outs
        ]
        names += [n for n, _ in outs] + ["factor_s", "phi_s"]
        results = pl.pallas_call(
            functools.partial(
                update_kernel, iteration, half, group, prep,
                sizes["item"], sizes["week"], n_arrived if iteration else 0, names,
            ),
            grid=(steps,),
            in_specs=in_specs,
            out_specs=out_specs,
            out_shape=[s for _, s in outs],
            scratch_shapes=[pltpu.VMEM((users, rank), F32)] * 2,
            compiler_params=pltpu.CompilerParams(vmem_limit_bytes=36 * 1024 * 1024),
            cost_estimate=pl.CostEstimate(
                flops=2 * 3 * users * weeks * items * 256,
                bytes_accessed=users * weeks * items,
                transcendentals=0,
            ),
        )(*[x for _, x in ins], *after)
        return dict(zip([n for n, _ in outs], results))

    chains = {}

    def advance(pair):
        parts, stage = chains[pair]
        x = tree(parts)
        chains[pair] = (exchange(x, *plan[stage]), stage + 1)
        return x

    def finish(pair):
        while chains[pair][1] < len(plan):
            advance(pair)
        return chains.pop(pair)[0]

    weights, small, factors = None, {}, {}
    den, previous, arrived = None, None, {}
    for iteration in range(ITERS):
        for pair in range(PAIRS):
            if iteration:
                arrived[pair] = finish(pair)
            for half in range(2):
                group = 2 * pair + half
                after = [] if previous is None else [previous]
                for other in sorted(chains):
                    if chains[other][1] < len(plan):
                        after.append(advance(other))
                ins = [("counts", counts if iteration == 0 else small[group]), ("week", week_factor)]
                outs = []
                if weights is None:
                    ins.append(("item_t", item_t))
                    outs += [
                        ("model_w", shape((4 * rank, items), BF16)),
                        ("phi_w", shape((items, 2 * rank), BF16)),
                    ]
                else:
                    ins += weights
                if iteration < 2:
                    ins.append(("factor_t", factor_t))
                else:
                    ins += [("factor", factors[group]), ("den", den)]
                if iteration:
                    ins += [("arrived%d" % k, a) for k, a in enumerate(arrived[pair])]
                    outs.append(("factor_out", shape((users, rank))))
                if iteration == 0:
                    outs.append(("small_out", shape((users, weeks, items), jnp.int8)))
                if iteration == 1:
                    outs.append(("den_out", shape((8, rank))))
                if half:
                    ins.append(("partner", previous))
                    rows = users + (8 if iteration == 0 else 0)
                    outs.append(("phi_out", shape((rows, 2 * rank))))
                else:
                    outs.append(("phi_out", shape((users, rank))))
                got = run(iteration, half, group, ins, outs, after)
                if weights is None:
                    weights = [("model_w", got["model_w"]), ("phi_w", got["phi_w"])]
                if iteration == 0:
                    small[group] = got["small_out"]
                else:
                    factors[group] = got["factor_out"]
                if iteration == 1:
                    den = got["den_out"]
                previous = got["phi_out"]
            chains[pair] = ([previous], 0)
    for pair in range(PAIRS):
        arrived[pair] = finish(pair)
    final_ins = [den]
    for pair in range(PAIRS):
        final_ins += [factors[2 * pair], factors[2 * pair + 1]] + arrived[pair]
    final = pl.pallas_call(
        functools.partial(last_kernel, n_arrived), out_shape=shape((rank, all_users))
    )(*final_ins)
    return final.T


def solution(mesh):
    axes = tuple(zip(mesh.axis_names, mesh.devices.shape))
    placed = (P(None, "week", "item"), P(), P("item", None), P("week", None))
    run = functools.partial(per_device, axes)
    return jax.shard_map(run, mesh=mesh, in_specs=placed, out_specs=P(), check_vma=False)
```

```python
import functools

import jax
import jax.numpy as jnp
from jax import lax
from jax.experimental import pallas as pl
from jax.experimental.pallas import tpu as pltpu
from jax.sharding import PartitionSpec as P

ITERS = 3
TILE_USERS = 8
SLOTS = 4
COLUMNS = 256
MOST = 7.0
ROUNDING = 2.8e-6
ALLOWED = 6.4e-9
F32, BF16 = jnp.float32, jnp.bfloat16


def split(x):
    high = x.astype(BF16)
    low = (x - high.astype(F32)).astype(BF16)
    return high, low


def sum_over(x, axes):
    for axis, size in axes:
        if size & (size - 1):
            x = lax.psum(x, axis)
            continue
        bit = 1
        while bit < size:
            x = x + lax.ppermute(x, axis, [(i, i ^ bit) for i in range(size)])
            bit *= 2
    return x


def spread(index, multiplier):
    return jnp.exp2(((index * multiplier) & 65535).astype(F32) * (1.0 / 65536.0))


def pack(x):
    half = x.shape[0] // 2
    return jnp.concatenate([x[:half], x[half:]], axis=1)


def unpack(x):
    rank = x.shape[1] // 2
    return jnp.concatenate([x[:, :rank], x[:, rank:]], axis=0)


def column_sums(item_t, week, n_item, n_week):
    rank, items = item_t.shape
    both = lax.dot_general(
        jnp.ones((8, items), BF16), jnp.concatenate(split(item_t), axis=0),
        (((1,), (1,)), ((), ())), preferred_element_type=F32,
    )
    sums = (both[:, :rank] + both[:, rank:]) * (1.0 / n_week)
    weeks = jnp.broadcast_to(jnp.sum(week, axis=0, keepdims=True), sums.shape) * (1.0 / n_item)
    return jnp.concatenate([sums, weeks], axis=1)


def update(factor, phi, den):
    new = factor * phi / den
    spread_sum = jnp.sum(jnp.sum(new / den, axis=0, keepdims=True), axis=1, keepdims=True)
    square_sum = jnp.sum(jnp.sum(new * new, axis=0, keepdims=True), axis=1, keepdims=True)
    sound = jnp.where((MOST * ROUNDING) * spread_sum <= ALLOWED * square_sum, 1.0, 0.0)
    return new, jnp.broadcast_to(sound, (8, 128))


def sweep_kernel(iteration, exact, axes, names, *refs):
    r = dict(zip(names, refs))
    counts, slots, arrived = r["counts"], r["slots"], r["arrived"]
    users, weeks, items = counts.shape
    rank = r["week"].shape[1]
    rows = TILE_USERS * weeks
    blocks = users // TILE_USERS
    model_w, phi_w, factor_s, week_s = r["model_w"], r["phi_w"], r["factor_s"], r["week_s"]

    def fetch(block, slot):
        at = pl.ds(pl.multiple_of(block * TILE_USERS, TILE_USERS), TILE_USERS)
        return pltpu.make_async_copy(counts.at[at], slots.at[slot], arrived.at[slot])

    for slot in range(min(SLOTS, blocks)):
        fetch(slot, slot).start()

    item_at = lax.broadcasted_iota(jnp.int32, (1, items), 1) + lax.axis_index("item") * items
    week_at = lax.broadcasted_iota(jnp.int32, (weeks, 1), 0) + lax.axis_index("week") * weeks
    item_t = r["item_t"][...] * spread(item_at, 40503)
    week_s[...] = r["week"][...] * spread(week_at, 27146)
    high, low = split(item_t)
    model_w[...] = jnp.concatenate([high, high, low, low], axis=0)
    phi_w[...] = jnp.concatenate([high.astype(F32), low.astype(F32)], axis=0).T.astype(BF16)

    if iteration == 0:
        factor_s[...] = r["factor_t"][...].T
    else:
        summed = r["summed"][...]
        if iteration == 1:
            sums = summed[users // 2:]
            den = sums[:, :rank] * sums[:, rank:]
            r["den_out"][...] = den
            old = r["factor_t"][...].T
        else:
            den = r["den"][...]
            old = r["factor"][...]
        new, sound = update(old, unpack(summed[: users // 2]), den[0:1, :])
        factor_s[...] = new
        r["factor_out"][...] = new
        r["sound_out"][...] = sound if iteration == 1 else sound * r["sound"][...]

    def operand(block):
        at = pl.ds(pl.multiple_of(block * TILE_USERS, TILE_USERS), TILE_USERS)
        scaled = factor_s[at, :][:, None, :] * week_s[...][None, :, :]
        high, low = split(scaled.reshape(rows, rank))
        return jnp.concatenate([high, low, high, low], axis=1)

    def model_of(lhs, start):
        return jnp.dot(lhs, model_w[:, start:start + COLUMNS], preferred_element_type=F32)

    r["lhs_s"][...] = operand(0)
    r["ahead_s"][...] = model_of(r["lhs_s"][...], 0)

    def body(block, carry):
        slot = lax.rem(block, SLOTS)
        fetch(block, slot).wait()
        lhs = r["lhs_s"][...]
        following = operand(jnp.minimum(block + 1, blocks - 1))
        ahead = r["ahead_s"][...]
        total = None
        for start in range(0, items, COLUMNS):
            model = ahead
            if start + COLUMNS < items:
                ahead = model_of(lhs, start + COLUMNS)
            else:
                r["ahead_s"][...] = model_of(following, 0)
                r["lhs_s"][...] = following
            count = slots[slot, :, :, start:start + COLUMNS].reshape(rows, COLUMNS)
            ratio = count.astype(F32) * pltpu.reciprocal(model, approx=True)
            rhs = phi_w[start:start + COLUMNS, :]
            if exact:
                ratio = jnp.concatenate(split(ratio), axis=1)
                rhs = jnp.concatenate([rhs, rhs], axis=0)
            else:
                ratio = ratio.astype(BF16)
            part = jnp.dot(ratio, rhs, preferred_element_type=F32)
            total = part if total is None else total + part
        total = (total[:, :rank] + total[:, rank:]).reshape(TILE_USERS, weeks, rank)
        at = pl.ds(pl.multiple_of(block * TILE_USERS, TILE_USERS), TILE_USERS)
        r["phi_s"][at, :] = jnp.sum(total * week_s[...][None, :, :], axis=1)

        @pl.when(block + SLOTS < blocks)
        def _():
            fetch(block + SLOTS, slot).start()

        return carry

    lax.fori_loop(0, blocks, body, 0)
    r["phi_out"][: users // 2, :] = pack(r["phi_s"][...])
    if iteration == 0:
        n_item, n_week = (dict(axes)[a] for a in ("item", "week"))
        r["phi_out"][users // 2:, :] = column_sums(r["item_t"][...], r["week"][...], n_item, n_week)


def last_kernel(factor, summed, den, sound, out, sound_out):
    new, fine = update(factor[...], unpack(summed[...]), den[0:1, :])
    out[...] = new.T
    sound_out[...] = (fine * sound[...]).astype(jnp.int32)


def updates(exact, axes, counts, user_factor, item_factor, week_factor):
    users, rank = user_factor.shape
    weeks, items = counts.shape[1:]
    rows = TILE_USERS * weeks
    factor_t, item_t = user_factor.T, item_factor.T
    travel = sorted(axes, reverse=True)

    def shape(dims, dtype=F32):
        return jax.ShapeDtypeStruct(dims, dtype)

    scratch = {
        "slots": pltpu.VMEM((SLOTS, TILE_USERS, weeks, items), jnp.int32),
        "arrived": pltpu.SemaphoreType.DMA((SLOTS,)),
        "model_w": pltpu.VMEM((4 * rank, items), BF16),
        "phi_w": pltpu.VMEM((items, 2 * rank), BF16),
        "factor_s": pltpu.VMEM((users, rank), F32),
        "week_s": pltpu.VMEM((weeks, rank), F32),
        "phi_s": pltpu.VMEM((users, rank), F32),
        "lhs_s": pltpu.VMEM((rows, 4 * rank), BF16),
        "ahead_s": pltpu.VMEM((rows, COLUMNS), F32),
    }

    def sweep(iteration, ins, outs):
        ins = {"counts": counts, "week": week_factor, "item_t": item_t, **ins}
        names = list(ins) + list(outs) + list(scratch)
        results = pl.pallas_call(
            functools.partial(sweep_kernel, iteration, exact, axes, names),
            in_specs=[
                pl.BlockSpec(memory_space=pl.ANY if n == "counts" else pltpu.VMEM) for n in ins
            ],
            out_specs=[pl.BlockSpec(memory_space=pltpu.VMEM)] * len(outs),
            out_shape=list(outs.values()),
            scratch_shapes=list(scratch.values()),
            compiler_params=pltpu.CompilerParams(vmem_limit_bytes=48 * 1024 * 1024),
            cost_estimate=pl.CostEstimate(
                flops=2 * (3 if exact else 2) * users * weeks * items * 256,
                bytes_accessed=4 * users * weeks * items,
                transcendentals=0,
            ),
        )(*ins.values())
        return dict(zip(outs, results))

    packed = shape((users // 2, 2 * rank))
    factor_out, sound_out = shape((users, rank)), shape((8, 128))
    got = sweep(0, {"factor_t": factor_t}, {"phi_out": shape((users // 2 + 8, 2 * rank))})
    summed = sum_over(got["phi_out"], travel)
    got = sweep(
        1, {"factor_t": factor_t, "summed": summed},
        {"phi_out": packed, "factor_out": factor_out, "sound_out": sound_out,
         "den_out": shape((8, rank))},
    )
    den = got["den_out"]
    for iteration in range(2, ITERS):
        got = sweep(
            iteration,
            {"factor": got["factor_out"], "summed": sum_over(got["phi_out"], travel),
             "den": den, "sound": got["sound_out"]},
            {"phi_out": packed, "factor_out": factor_out, "sound_out": sound_out},
        )
    out, sound = pl.pallas_call(
        last_kernel, out_shape=[shape((rank, users)), shape((8, 128), jnp.int32)]
    )(got["factor_out"], sum_over(got["phi_out"], travel), den, got["sound_out"])
    return out.T, sound[0, 0]


def per_device(axes, *arrays):
    out, sound = updates(False, axes, *arrays)
    return lax.cond(sound == 1, lambda *_: out, lambda *a: updates(True, axes, *a)[0], *arrays)


def solution(mesh):
    axes = tuple(zip(mesh.axis_names, mesh.devices.shape))
    placed = (P(None, "week", "item"), P(), P("item", None), P("week", None))
    run = functools.partial(per_device, axes)
    return jax.shard_map(run, mesh=mesh, in_specs=placed, out_specs=P(), check_vma=False)
```

```python
import functools

import jax
import jax.numpy as jnp
from jax import lax
from jax.experimental import pallas as pl
from jax.experimental.pallas import tpu as pltpu
from jax.sharding import PartitionSpec as P

ITERS = 3
TILE_USERS = 8
SLOTS = 4
COLUMNS = 256
GROUP = 4
MOST = 7.0
ROUNDING = 2.8e-6
ALLOWED = 6.4e-9
F32, BF16 = jnp.float32, jnp.bfloat16


def split(x):
    high = x.astype(BF16)
    low = (x - high.astype(F32)).astype(BF16)
    return high, low


def sum_over(x, axes):
    for axis, size in axes:
        if size & (size - 1):
            x = lax.psum(x, axis)
            continue
        left = size
        while left > 1:
            width = min(GROUP, left)
            left //= width
            parts = [x]
            for k in range(1, width):
                partners = [(i, i ^ (k * left)) for i in range(size)]
                parts.append(lax.ppermute(x, axis, partners))
            while len(parts) > 1:
                parts = [p + q for p, q in zip(parts[0::2], parts[1::2])]
            x = parts[0]
    return x


def spread(index, multiplier):
    return jnp.exp2(((index * multiplier) & 65535).astype(F32) * (1.0 / 65536.0))


def pack(x):
    half = x.shape[0] // 2
    return jnp.concatenate([x[:half], x[half:]], axis=1)


def unpack(x):
    rank = x.shape[1] // 2
    return jnp.concatenate([x[:, :rank], x[:, rank:]], axis=0)


def column_sums(item_t, week, n_item, n_week):
    rank, items = item_t.shape
    both = lax.dot_general(
        jnp.ones((8, items), BF16), jnp.concatenate(split(item_t), axis=0),
        (((1,), (1,)), ((), ())), preferred_element_type=F32,
    )
    sums = (both[:, :rank] + both[:, rank:]) * (1.0 / n_week)
    weeks = jnp.broadcast_to(jnp.sum(week, axis=0, keepdims=True), sums.shape) * (1.0 / n_item)
    return jnp.concatenate([sums, weeks], axis=1)


def update(factor, phi, den):
    new = factor * phi / den
    spread_sum = jnp.sum(jnp.sum(new / den, axis=0, keepdims=True), axis=1, keepdims=True)
    square_sum = jnp.sum(jnp.sum(new * new, axis=0, keepdims=True), axis=1, keepdims=True)
    sound = jnp.where((MOST * ROUNDING) * spread_sum <= ALLOWED * square_sum, 1.0, 0.0)
    return new, jnp.broadcast_to(sound, (8, 128))


def sweep_kernel(iteration, exact, axes, names, *refs):
    r = dict(zip(names, refs))
    counts = r["counts"]
    users, weeks, items = counts.shape
    first = iteration == 0
    rank = r["week"].shape[1]
    rows = TILE_USERS * weeks
    blocks = users // TILE_USERS
    model_w, phi_w, factor_s, week_s = r["model_w"], r["phi_w"], r["factor_s"], r["week_s"]

    def users_of(block):
        return pl.ds(pl.multiple_of(block * TILE_USERS, TILE_USERS), TILE_USERS)

    def fetch(block, slot):
        return pltpu.make_async_copy(
            counts.at[users_of(block)], r["slots"].at[slot], r["arrived"].at[slot]
        )

    if first:
        for slot in range(min(SLOTS, blocks)):
            fetch(slot, slot).start()

    item_at = lax.broadcasted_iota(jnp.int32, (1, items), 1) + lax.axis_index("item") * items
    week_at = lax.broadcasted_iota(jnp.int32, (weeks, 1), 0) + lax.axis_index("week") * weeks
    item_t = r["item_t"][...] * spread(item_at, 40503)
    week_s[...] = r["week"][...] * spread(week_at, 27146)
    high, low = split(item_t)
    model_w[...] = jnp.concatenate([high, high, low, low], axis=0)
    phi_w[...] = jnp.concatenate([high.astype(F32), low.astype(F32)], axis=0).T.astype(BF16)

    if first:
        factor_s[...] = r["factor_t"][...].T
    else:
        summed = r["summed"][...]
        if iteration == 1:
            sums = summed[users // 2:]
            den = sums[:, :rank] * sums[:, rank:]
            r["den_out"][...] = den
            old = r["factor_t"][...].T
        else:
            den = r["den"][...]
            old = r["factor"][...]
        new, sound = update(old, unpack(summed[: users // 2]), den[0:1, :])
        factor_s[...] = new
        r["factor_out"][...] = new
        r["sound_out"][...] = sound if iteration == 1 else sound * r["sound"][...]

    def operand(block):
        scaled = factor_s[users_of(block), :][:, None, :] * week_s[...][None, :, :]
        high, low = split(scaled.reshape(rows, rank))
        return jnp.concatenate([high, low, high, low], axis=1)

    def model_of(lhs, start):
        return jnp.dot(lhs, model_w[:, start:start + COLUMNS], preferred_element_type=F32)

    r["lhs_s"][...] = operand(0)
    r["ahead_s"][...] = model_of(r["lhs_s"][...], 0)

    def body(block, carry):
        slot = lax.rem(block, SLOTS)
        if first:
            fetch(block, slot).wait()
        lhs = r["lhs_s"][...]
        following = operand(jnp.minimum(block + 1, blocks - 1))
        ahead = r["ahead_s"][...]
        total = None
        for start in range(0, items, COLUMNS):
            model = ahead
            if start + COLUMNS < items:
                ahead = model_of(lhs, start + COLUMNS)
            else:
                r["ahead_s"][...] = model_of(following, 0)
                r["lhs_s"][...] = following
            at = slice(start, start + COLUMNS)
            if first:
                count = r["slots"][slot, :, :, at]
                r["small_out"][users_of(block), :, at] = count.astype(jnp.int8)
            else:
                count = counts[users_of(block), :, at].astype(jnp.int32)
            count = count.astype(F32).reshape(rows, COLUMNS)
            ratio = count * pltpu.reciprocal(model, approx=True, full_range=False)
            rhs = phi_w[at, :]
            if exact:
                ratio = jnp.concatenate(split(ratio), axis=1)
                rhs = jnp.concatenate([rhs, rhs], axis=0)
            else:
                ratio = ratio.astype(BF16)
            part = jnp.dot(ratio, rhs, preferred_element_type=F32)
            total = part if total is None else total + part
        total = (total[:, :rank] + total[:, rank:]).reshape(TILE_USERS, weeks, rank)
        r["phi_s"][users_of(block), :] = jnp.sum(total * week_s[...][None, :, :], axis=1)

        if first:

            @pl.when(block + SLOTS < blocks)
            def _():
                fetch(block + SLOTS, slot).start()

        return carry

    lax.fori_loop(0, blocks, body, 0)
    r["phi_out"][: users // 2, :] = pack(r["phi_s"][...])
    if first:
        n_item, n_week = (dict(axes)[a] for a in ("item", "week"))
        r["phi_out"][users // 2:, :] = column_sums(r["item_t"][...], r["week"][...], n_item, n_week)


def last_kernel(factor, summed, den, sound, out, sound_out):
    new, fine = update(factor[...], unpack(summed[...]), den[0:1, :])
    out[...] = new.T
    sound_out[...] = (fine * sound[...]).astype(jnp.int32)


def updates(exact, axes, counts, user_factor, item_factor, week_factor):
    users, rank = user_factor.shape
    weeks, items = counts.shape[1:]
    rows = TILE_USERS * weeks
    factor_t, item_t = user_factor.T, item_factor.T
    travel = sorted(axes, reverse=True)

    def shape(dims, dtype=F32):
        return jax.ShapeDtypeStruct(dims, dtype)

    stream = {
        "slots": pltpu.VMEM((SLOTS, TILE_USERS, weeks, items), jnp.int32),
        "arrived": pltpu.SemaphoreType.DMA((SLOTS,)),
    }
    scratch = {
        "model_w": pltpu.VMEM((4 * rank, items), BF16),
        "phi_w": pltpu.VMEM((items, 2 * rank), BF16),
        "factor_s": pltpu.VMEM((users, rank), F32),
        "week_s": pltpu.VMEM((weeks, rank), F32),
        "phi_s": pltpu.VMEM((users, rank), F32),
        "lhs_s": pltpu.VMEM((rows, 4 * rank), BF16),
        "ahead_s": pltpu.VMEM((rows, COLUMNS), F32),
    }

    def sweep(iteration, counts, ins, outs):
        ins = {"counts": counts, "week": week_factor, "item_t": item_t, **ins}
        first = iteration == 0
        scratches = {**stream, **scratch} if first else scratch
        names = list(ins) + list(outs) + list(scratches)
        results = pl.pallas_call(
            functools.partial(sweep_kernel, iteration, exact, axes, names),
            in_specs=[
                pl.BlockSpec(memory_space=pl.ANY if first and n == "counts" else pltpu.VMEM)
                for n in ins
            ],
            out_specs=[pl.BlockSpec(memory_space=pltpu.VMEM)] * len(outs),
            out_shape=list(outs.values()),
            scratch_shapes=list(scratches.values()),
            compiler_params=pltpu.CompilerParams(vmem_limit_bytes=(30 if first else 16) * 1024 * 1024),
            cost_estimate=pl.CostEstimate(
                flops=2 * (3 if exact else 2) * users * weeks * items * 256,
                bytes_accessed=4 * users * weeks * items,
                transcendentals=0,
            ),
        )(*ins.values())
        return dict(zip(outs, results))

    packed = shape((users // 2, 2 * rank))
    factor_out, sound_out = shape((users, rank)), shape((8, 128))
    got = sweep(
        0, counts, {"factor_t": factor_t},
        {"phi_out": shape((users // 2 + 8, 2 * rank)), "small_out": shape(counts.shape, jnp.int8)},
    )
    small = got["small_out"]
    summed = sum_over(got["phi_out"], travel)
    got = sweep(
        1, small, {"factor_t": factor_t, "summed": summed},
        {"phi_out": packed, "factor_out": factor_out, "sound_out": sound_out,
         "den_out": shape((8, rank))},
    )
    den = got["den_out"]
    for iteration in range(2, ITERS):
        got = sweep(
            iteration, small,
            {"factor": got["factor_out"], "summed": sum_over(got["phi_out"], travel),
             "den": den, "sound": got["sound_out"]},
            {"phi_out": packed, "factor_out": factor_out, "sound_out": sound_out},
        )
    out, sound = pl.pallas_call(
        last_kernel, out_shape=[shape((rank, users)), shape((8, 128), jnp.int32)]
    )(got["factor_out"], sum_over(got["phi_out"], travel), den, got["sound_out"])
    return out.T, sound[0, 0]


def per_device(axes, *arrays):
    out, sound = updates(False, axes, *arrays)
    return lax.cond(sound == 1, lambda *_: out, lambda *a: updates(True, axes, *a)[0], *arrays)


def solution(mesh):
    axes = tuple(zip(mesh.axis_names, mesh.devices.shape))
    placed = (P(None, "week", "item"), P(), P("item", None), P("week", None))
    run = functools.partial(per_device, axes)
    return jax.shard_map(run, mesh=mesh, in_specs=placed, out_specs=P(), check_vma=False)
```

```python
import functools

import jax
import jax.numpy as jnp
from jax import lax
from jax.experimental import pallas as pl
from jax.experimental.pallas import tpu as pltpu
from jax.sharding import PartitionSpec as P

ITERS = 3
TILE_USERS = 8
SLOTS = 4
COLUMNS = 256
STRIP = 64
GROUP = 4
MOST = 7.0
ROUNDING = 2.8e-6
ALLOWED = 6.4e-9
F32, BF16 = jnp.float32, jnp.bfloat16


def split(x):
    high = x.astype(BF16)
    low = (x - high.astype(F32)).astype(BF16)
    return high, low


def sum_over(x, axes):
    for axis, size in axes:
        if size & (size - 1):
            x = lax.psum(x, axis)
            continue
        left = size
        while left > 1:
            width = min(GROUP, left)
            left //= width
            parts = [x]
            for k in range(1, width):
                partners = [(i, i ^ (k * left)) for i in range(size)]
                parts.append(lax.ppermute(x, axis, partners))
            while len(parts) > 1:
                parts = [p + q for p, q in zip(parts[0::2], parts[1::2])]
            x = parts[0]
    return x


def spread(index, multiplier):
    return jnp.exp2(((index * multiplier) & 65535).astype(F32) * (1.0 / 65536.0))


def pack(x):
    half = x.shape[0] // 2
    return jnp.concatenate([x[:half], x[half:]], axis=1)


def unpack(x):
    rank = x.shape[1] // 2
    return jnp.concatenate([x[:, :rank], x[:, rank:]], axis=0)


def column_sums(item_t, week, n_item, n_week):
    rank = item_t.shape[0]
    sums = jnp.broadcast_to(jnp.sum(item_t, axis=1, keepdims=True), (rank, 128)).T[:8]
    sums = sums * (1.0 / n_week)
    weeks = jnp.broadcast_to(jnp.sum(week, axis=0, keepdims=True), sums.shape) * (1.0 / n_item)
    return jnp.concatenate([sums, weeks], axis=1)


def update(factor, phi, den):
    new = factor * phi / den
    spread_sum = jnp.sum(jnp.sum(new / den, axis=0, keepdims=True), axis=1, keepdims=True)
    square_sum = jnp.sum(jnp.sum(new * new, axis=0, keepdims=True), axis=1, keepdims=True)
    sound = jnp.where((MOST * ROUNDING) * spread_sum <= ALLOWED * square_sum, 1.0, 0.0)
    return new, jnp.broadcast_to(sound, (8, 128))


def sweep_kernel(iteration, exact, axes, names, units, *refs):
    r = dict(zip(names, refs))
    counts = r["counts"]
    users, weeks, items = counts.shape
    first = iteration == 0
    rank = r["week"].shape[1]
    rows = TILE_USERS * weeks
    blocks = users // TILE_USERS
    model_w, phi_w, factor_s, week_s = r["model_w"], r["phi_w"], r["factor_s"], r["week_s"]

    def users_of(block):
        return pl.ds(pl.multiple_of(block * TILE_USERS, TILE_USERS), TILE_USERS)

    def fetch(block, slot):
        return pltpu.make_async_copy(
            counts.at[users_of(block)], r["slots"].at[slot], r["arrived"].at[slot]
        )

    if first:
        for slot in range(min(SLOTS, blocks)):
            fetch(slot, slot).start()

    item_at = lax.broadcasted_iota(jnp.int32, (1, items), 1) + lax.axis_index("item") * items
    week_at = lax.broadcasted_iota(jnp.int32, (weeks, 1), 0) + lax.axis_index("week") * weeks
    item_t = r["item_t"][...] * spread(item_at, 40503)
    week_s[...] = r["week"][...] * spread(week_at, 27146)
    high, low = split(item_t)
    model_w[...] = jnp.concatenate([high, high, low, low], axis=0)
    phi_w[:, : 2 * rank] = jnp.concatenate(
        [high.astype(F32), low.astype(F32)], axis=0
    ).T.astype(BF16)
    phi_w[:, 2 * rank:] = jnp.zeros((items, COLUMNS - 2 * rank), BF16)

    if first:
        factor_s[...] = r["factor_t"][...].T
    else:
        summed = r["summed"][...]
        if iteration == 1:
            sums = summed[users // 2:]
            den = sums[:, :rank] * sums[:, rank:]
            r["den_out"][...] = den
            old = r["factor_t"][...].T
        else:
            den = r["den"][...]
            old = r["factor"][...]
        new, sound = update(old, unpack(summed[: users // 2]), den[0:1, :])
        factor_s[...] = new
        r["factor_out"][...] = new
        r["sound_out"][...] = sound if iteration == 1 else sound * r["sound"][...]

    def operand(block):
        scaled = factor_s[users_of(block), :][:, None, :] * week_s[...][None, :, :]
        high, low = split(scaled.reshape(rows, rank))
        return jnp.concatenate([high, low, high, low], axis=1)

    strips = [slice(at, at + STRIP) for at in range(0, rows, STRIP)]
    chunks = items // COLUMNS
    lhs_s = r["lhs_s"]

    def push_model(chunk):
        at = pl.ds(chunk % chunks * COLUMNS, COLUMNS)
        pltpu.matmul_push_rhs(model_w[:, at], 0, 0)

    def push_phi(chunk):
        at = pl.ds(chunk % chunks * COLUMNS, COLUMNS)
        pltpu.matmul_push_rhs(phi_w[at, :], 0, 1)

    def matmuls(even, odd, total):
        ahead = (even, odd)
        lhs_s[0] = operand(0)
        push_model(0)
        for n, strip in enumerate(strips):
            pltpu.matmul_acc_lhs(ahead[0][n], lhs_s[0, strip, :], None if n else 0)
        push_model(1)
        push_phi(0)

        def body(block, carry):
            slot = lax.rem(block, SLOTS)
            if first:
                fetch(block, slot).wait()
            this, other = lax.rem(block, 2), lax.rem(block + 1, 2)
            lhs_s[other] = operand(jnp.minimum(block + 1, blocks - 1))
            for chunk in range(chunks):
                source = this if chunk + 1 < chunks else other
                at = slice(chunk * COLUMNS, (chunk + 1) * COLUMNS)
                for n, strip in enumerate(strips):
                    staged = None if n else 0
                    pltpu.matmul_acc_lhs(ahead[(chunk + 1) % 2][n], lhs_s[source, strip, :], staged)
                    model = pltpu.matmul_pop(ahead[chunk % 2][n])
                    user, week = divmod(strip.start, weeks)
                    some = slice(user, user + max(1, STRIP // weeks))
                    part = slice(week, week + min(STRIP, weeks))
                    if first:
                        count = r["slots"][slot, some, part, at]
                        mine = pl.ds(block * TILE_USERS + some.start, some.stop - some.start)
                        r["small_out"][mine, part, at] = count.astype(jnp.int8)
                    else:
                        mine = pl.ds(block * TILE_USERS + some.start, some.stop - some.start)
                        count = counts[mine, part, at].astype(jnp.int32)
                    count = count.astype(F32).reshape(STRIP, COLUMNS)
                    ratio = count * pltpu.reciprocal(model, approx=True, full_range=False)
                    if exact:
                        high, low = split(ratio)
                        pltpu.matmul_acc_lhs(total[n], high, staged)
                        pltpu.matmul_acc_lhs(total[n], low)
                    else:
                        pltpu.matmul_acc_lhs(total[n], ratio.astype(BF16), staged)
                    if n == len(strips) // 2:
                        push_model(chunk + 2)
                        push_phi(chunk + 1)
            sums = jnp.concatenate([pltpu.matmul_pop(t) for t in total], axis=0)
            sums = (sums[:, :rank] + sums[:, rank: 2 * rank]).reshape(TILE_USERS, weeks, rank)
            r["phi_s"][users_of(block), :] = jnp.sum(sums * week_s[...][None, :, :], axis=1)
            if first:

                @pl.when(block + SLOTS < blocks)
                def _():
                    fetch(block + SLOTS, slot).start()

            return carry

        lax.fori_loop(0, blocks, body, 0)
        nothing = jnp.zeros((STRIP, COLUMNS), BF16)
        pltpu.matmul_acc_lhs(ahead[1][0], nothing, 0)
        pltpu.matmul_acc_lhs(total[0], nothing, 0)
        for ref in ahead[0] + [ahead[1][0], total[0]]:
            pltpu.matmul_pop(ref)

    pl.run_scoped(matmuls, *[[unit] * len(strips) for unit in units])
    r["phi_out"][: users // 2, :] = pack(r["phi_s"][...])
    if first:
        n_item, n_week = (dict(axes)[a] for a in ("item", "week"))
        r["phi_out"][users // 2:, :] = column_sums(r["item_t"][...], r["week"][...], n_item, n_week)


def last_kernel(factor, summed, den, sound, out, sound_out):
    new, fine = update(factor[...], unpack(summed[...]), den[0:1, :])
    out[...] = new.T
    sound_out[...] = (fine * sound[...]).astype(jnp.int32)


def updates(exact, mesh, axes, counts, user_factor, item_factor, week_factor):
    users, rank = user_factor.shape
    weeks, items = counts.shape[1:]
    rows = TILE_USERS * weeks
    factor_t, item_t = user_factor.T, item_factor.T
    travel = sorted(axes, reverse=True)

    def shape(dims, dtype=F32):
        return jax.ShapeDtypeStruct(dims, dtype)

    stream = {
        "slots": pltpu.VMEM((SLOTS, TILE_USERS, weeks, items), jnp.int32),
        "arrived": pltpu.SemaphoreType.DMA((SLOTS,)),
    }
    scratch = {
        "model_w": pltpu.VMEM((4 * rank, items), BF16),
        "phi_w": pltpu.VMEM((items, COLUMNS), BF16),
        "factor_s": pltpu.VMEM((users, rank), F32),
        "week_s": pltpu.VMEM((weeks, rank), F32),
        "phi_s": pltpu.VMEM((users, rank), F32),
        "lhs_s": pltpu.VMEM((2, rows, 4 * rank), BF16),
    }
    with jax.sharding.use_abstract_mesh(mesh.abstract_mesh):
        units = [pltpu.ACC(unit)((STRIP, COLUMNS), F32) for unit in (0, 0, 1)]

    def sweep(iteration, counts, ins, outs):
        ins = {"counts": counts, "week": week_factor, "item_t": item_t, **ins}
        first = iteration == 0
        scratches = {**stream, **scratch} if first else scratch
        names = list(ins) + list(outs) + list(scratches)
        results = pl.pallas_call(
            functools.partial(sweep_kernel, iteration, exact, axes, names, units),
            in_specs=[
                pl.BlockSpec(memory_space=pl.ANY if first and n == "counts" else pltpu.VMEM)
                for n in ins
            ],
            out_specs=[pl.BlockSpec(memory_space=pltpu.VMEM)] * len(outs),
            out_shape=list(outs.values()),
            scratch_shapes=list(scratches.values()),
            compiler_params=pltpu.CompilerParams(vmem_limit_bytes=(30 if first else 16) * 1024 * 1024),
            cost_estimate=pl.CostEstimate(
                flops=2 * (3 if exact else 2) * users * weeks * items * 256,
                bytes_accessed=4 * users * weeks * items,
                transcendentals=0,
            ),
        )(*ins.values())
        return dict(zip(outs, results))

    packed = shape((users // 2, 2 * rank))
    factor_out, sound_out = shape((users, rank)), shape((8, 128))
    got = sweep(
        0, counts, {"factor_t": factor_t},
        {"phi_out": shape((users // 2 + 8, 2 * rank)), "small_out": shape(counts.shape, jnp.int8)},
    )
    small = got["small_out"]
    summed = sum_over(got["phi_out"], travel)
    got = sweep(
        1, small, {"factor_t": factor_t, "summed": summed},
        {"phi_out": packed, "factor_out": factor_out, "sound_out": sound_out,
         "den_out": shape((8, rank))},
    )
    den = got["den_out"]
    for iteration in range(2, ITERS):
        got = sweep(
            iteration, small,
            {"factor": got["factor_out"], "summed": sum_over(got["phi_out"], travel),
             "den": den, "sound": got["sound_out"]},
            {"phi_out": packed, "factor_out": factor_out, "sound_out": sound_out},
        )
    out, sound = pl.pallas_call(
        last_kernel, out_shape=[shape((rank, users)), shape((8, 128), jnp.int32)]
    )(got["factor_out"], sum_over(got["phi_out"], travel), den, got["sound_out"])
    return out.T, sound[0, 0]


def per_device(mesh, axes, *arrays):
    out, sound = updates(False, mesh, axes, *arrays)
    return lax.cond(sound == 1, lambda *_: out, lambda *a: updates(True, mesh, axes, *a)[0], *arrays)


def solution(mesh):
    axes = tuple(zip(mesh.axis_names, mesh.devices.shape))
    placed = (P(None, "week", "item"), P(), P("item", None), P("week", None))
    run = functools.partial(per_device, mesh, axes)
    return jax.shard_map(run, mesh=mesh, in_specs=placed, out_specs=P(), check_vma=False)
```

```python
import functools

import jax
import jax.numpy as jnp
from jax import lax
from jax.experimental import pallas as pl
from jax.experimental.pallas import tpu as pltpu
from jax.sharding import PartitionSpec as P

ITERS = 3
TILE_USERS = 16
FETCH_USERS = 8
SLOTS = 4
COLUMNS = 256
GROUP = 4
MOST = 7.0
ROUNDING = 2.8e-6
ALLOWED = 6.4e-9
F32, BF16 = jnp.float32, jnp.bfloat16


def split(x):
    high = x.astype(BF16)
    low = (x - high.astype(F32)).astype(BF16)
    return high, low


def sum_over(x, axes):
    for axis, size in axes:
        if size & (size - 1):
            x = lax.psum(x, axis)
            continue
        left = size
        while left > 1:
            width = min(GROUP, left)
            left //= width
            parts = [x]
            for k in range(1, width):
                partners = [(i, i ^ (k * left)) for i in range(size)]
                parts.append(lax.ppermute(x, axis, partners))
            while len(parts) > 1:
                parts = [p + q for p, q in zip(parts[0::2], parts[1::2])]
            x = parts[0]
    return x


def spread(index, multiplier):
    return jnp.exp2(((index * multiplier) & 65535).astype(F32) * (1.0 / 65536.0))


def pack(x):
    half = x.shape[0] // 2
    return jnp.concatenate([x[:half], x[half:]], axis=1)


def unpack(x):
    rank = x.shape[1] // 2
    return jnp.concatenate([x[:, :rank], x[:, rank:]], axis=0)


def column_sums(item_t, week, n_item, n_week):
    rank = item_t.shape[0]
    sums = jnp.broadcast_to(jnp.sum(item_t, axis=1, keepdims=True), (rank, 128)).T[:8]
    sums = sums * (1.0 / n_week)
    weeks = jnp.broadcast_to(jnp.sum(week, axis=0, keepdims=True), sums.shape) * (1.0 / n_item)
    return jnp.concatenate([sums, weeks], axis=1)


def update(factor, phi, den):
    new = factor * phi / den
    spread_sum = jnp.sum(jnp.sum(new / den, axis=0, keepdims=True), axis=1, keepdims=True)
    square_sum = jnp.sum(jnp.sum(new * new, axis=0, keepdims=True), axis=1, keepdims=True)
    sound = jnp.where((MOST * ROUNDING) * spread_sum <= ALLOWED * square_sum, 1.0, 0.0)
    return new, jnp.broadcast_to(sound, (8, 128))


def sweep_kernel(iteration, exact, axes, names, units, *refs):
    r = dict(zip(names, refs))
    counts = r["counts"]
    users, weeks, items = counts.shape
    first = iteration == 0
    rank = r["week"].shape[1]
    rows = TILE_USERS * weeks
    blocks = users // TILE_USERS
    halves = TILE_USERS // FETCH_USERS
    model_w, phi_w, factor_s, week_s = r["model_w"], r["phi_w"], r["factor_s"], r["week_s"]

    def fetch(part):
        at = pl.ds(pl.multiple_of(part * FETCH_USERS, FETCH_USERS), FETCH_USERS)
        slot = lax.rem(part, SLOTS)
        return pltpu.make_async_copy(
            counts.at[at], r["slots"].at[slot], r["arrived"].at[slot]
        )

    week_at = lax.broadcasted_iota(jnp.int32, (weeks, 1), 0) + lax.axis_index("week") * weeks
    week_s[...] = r["week"][...] * spread(week_at, 27146)

    if first:
        for part in range(min(SLOTS, users // FETCH_USERS)):
            fetch(jnp.int32(part)).start()
        item_at = lax.broadcasted_iota(jnp.int32, (1, items), 1)
        item_at = item_at + lax.axis_index("item") * items
        high, low = split(r["item_t"][...] * spread(item_at, 40503))
        model_w[...] = jnp.concatenate([high, high, low, low], axis=0)
        phi_w[:, : 2 * rank] = jnp.concatenate(
            [high.astype(F32), low.astype(F32)], axis=0
        ).T.astype(BF16)
        phi_w[:, 2 * rank:] = jnp.zeros((items, COLUMNS - 2 * rank), BF16)
        factor_s[...] = r["factor_t"][...].T
    else:
        summed = r["summed"][...]
        if iteration == 1:
            sums = summed[users // 2:]
            den = sums[:, :rank] * sums[:, rank:]
            r["den_out"][...] = den
            old = r["factor_t"][...].T
        else:
            den = r["den"][...]
            old = r["factor"][...]
        new, sound = update(old, unpack(summed[: users // 2]), den[0:1, :])
        factor_s[...] = new
        r["factor_out"][...] = new
        r["sound_out"][...] = sound if iteration == 1 else sound * r["sound"][...]

    strips = [slice(n * weeks, (n + 1) * weeks) for n in range(TILE_USERS)]
    chunks = items // COLUMNS
    lhs_s, phi_s = r["lhs_s"], r["phi_s"]

    def operand(user):
        high, low = split(factor_s[pl.ds(user, 1), :] * week_s[...])
        return jnp.concatenate([high, low, high, low], axis=1)

    def push_model(chunk):
        at = pl.ds(chunk % chunks * COLUMNS, COLUMNS)
        pltpu.matmul_push_rhs(model_w[:, at], 0, 0)

    def push_phi(chunk):
        at = pl.ds(chunk % chunks * COLUMNS, COLUMNS)
        pltpu.matmul_push_rhs(phi_w[at, :], 0, 1)

    def matmuls(ahead, total):
        def keep(n, user):
            sums = pltpu.matmul_pop(total[n])
            sums = (sums[:, :rank] + sums[:, rank: 2 * rank]) * week_s[...]
            phi_s[pl.ds(user, 1), :] = jnp.sum(sums, axis=0, keepdims=True)

        push_model(0)
        for n, strip in enumerate(strips):
            lhs_s[strip, :] = operand(n)
            pltpu.matmul_acc_lhs(ahead[n], lhs_s[strip, :], None if n else 0)
        push_model(1)
        push_phi(0)

        def body(block, carry):
            start = block * TILE_USERS
            before = lax.rem(start + users - TILE_USERS, users)
            after = jnp.minimum(start + TILE_USERS, users - TILE_USERS)
            for chunk in range(chunks):
                at = slice(chunk * COLUMNS, (chunk + 1) * COLUMNS)
                for n, strip in enumerate(strips):
                    part = block * halves + n // FETCH_USERS
                    if first and chunk == 0 and n % FETCH_USERS == 0:
                        fetch(part).wait()
                    staged = None if n else 0
                    model = pltpu.matmul_pop(ahead[n])
                    if chunk + 1 < chunks:
                        pltpu.matmul_acc_lhs(ahead[n], lhs_s[strip, :], staged)
                    else:
                        following = operand(after + n)
                        lhs_s[strip, :] = following
                        pltpu.matmul_acc_lhs(ahead[n], following, staged)
                    if first:
                        count = r["slots"][lax.rem(part, SLOTS), n % FETCH_USERS, :, at]
                        r["small_out"][start + n, :, at] = count.astype(jnp.int8)
                    else:
                        count = counts[start + n, :, at].astype(jnp.int32)
                    ratio = count.astype(F32) * pltpu.reciprocal(
                        model, approx=True, full_range=False
                    )
                    if chunk == 0:
                        keep(n, before + n)
                    if exact:
                        high, low = split(ratio)
                        pltpu.matmul_acc_lhs(total[n], high, staged)
                        pltpu.matmul_acc_lhs(total[n], low)
                    else:
                        pltpu.matmul_acc_lhs(total[n], ratio.astype(BF16), staged)
                    if n == len(strips) // 2:
                        push_model(chunk + 2)
                        push_phi(chunk + 1)
            if first:

                @pl.when((block + 1) * halves + SLOTS <= users // FETCH_USERS)
                def _():
                    for half in range(halves):
                        fetch(block * halves + SLOTS + half).start()

            return carry

        lax.fori_loop(0, blocks, body, 0)
        for n in range(TILE_USERS):
            keep(n, users - TILE_USERS + n)
        nothing = jnp.zeros((weeks, COLUMNS), BF16)
        for ref in ahead:
            pltpu.matmul_pop(ref)
        for ref in (ahead[0], total[0]):
            pltpu.matmul_acc_lhs(ref, nothing, 0)
            pltpu.matmul_pop(ref)

    pl.run_scoped(matmuls, *[[unit] * TILE_USERS for unit in units])
    r["phi_out"][: users // 2, :] = pack(phi_s[...])
    if first:
        n_item, n_week = (dict(axes)[a] for a in ("item", "week"))
        r["phi_out"][users // 2:, :] = column_sums(r["item_t"][...], r["week"][...], n_item, n_week)


def last_kernel(factor, summed, den, sound, out, sound_out):
    new, fine = update(factor[...], unpack(summed[...]), den[0:1, :])
    out[...] = new.T
    sound_out[0] = jnp.min(fine * sound[...]).astype(jnp.int32)


def updates(exact, mesh, axes, counts, user_factor, item_factor, week_factor):
    users, rank = user_factor.shape
    weeks, items = counts.shape[1:]
    rows = TILE_USERS * weeks
    factor_t, item_t = user_factor.T, item_factor.T
    travel = sorted(axes, reverse=True)

    def shape(dims, dtype=F32):
        return jax.ShapeDtypeStruct(dims, dtype)

    stream = {
        "slots": pltpu.VMEM((SLOTS, FETCH_USERS, weeks, items), jnp.int32),
        "arrived": pltpu.SemaphoreType.DMA((SLOTS,)),
    }
    scratch = {
        "factor_s": pltpu.VMEM((users, rank), F32),
        "week_s": pltpu.VMEM((weeks, rank), F32),
        "phi_s": pltpu.VMEM((users, rank), F32),
        "lhs_s": pltpu.VMEM((rows, 4 * rank), BF16),
    }
    with jax.sharding.use_abstract_mesh(mesh.abstract_mesh):
        units = [pltpu.ACC(unit)((weeks, COLUMNS), F32) for unit in (0, 1)]

    def sweep(iteration, counts, ins, outs):
        ins = {"counts": counts, "week": week_factor, **ins}
        first = iteration == 0
        scratches = {**stream, **scratch} if first else scratch
        names = list(ins) + list(outs) + list(scratches)
        results = pl.pallas_call(
            functools.partial(sweep_kernel, iteration, exact, axes, names, units),
            in_specs=[
                pl.BlockSpec(memory_space=pl.ANY if first and n == "counts" else pltpu.VMEM)
                for n in ins
            ],
            out_specs=[pl.BlockSpec(memory_space=pltpu.VMEM)] * len(outs),
            out_shape=list(outs.values()),
            scratch_shapes=list(scratches.values()),
            compiler_params=pltpu.CompilerParams(vmem_limit_bytes=(22 if first else 8) * 1024 * 1024),
            cost_estimate=pl.CostEstimate(
                flops=2 * (3 if exact else 2) * users * weeks * items * 256,
                bytes_accessed=4 * users * weeks * items,
                transcendentals=0,
            ),
        )(*ins.values())
        return dict(zip(outs, results))

    packed = shape((users // 2, 2 * rank))
    factor_out, sound_out = shape((users, rank)), shape((8, 128))
    got = sweep(
        0, counts, {"factor_t": factor_t, "item_t": item_t},
        {"phi_out": shape((users // 2 + 8, 2 * rank)), "small_out": shape(counts.shape, jnp.int8),
         "model_w": shape((4 * rank, items), BF16), "phi_w": shape((items, COLUMNS), BF16)},
    )
    small, weights = got["small_out"], {n: got[n] for n in ("model_w", "phi_w")}
    summed = sum_over(got["phi_out"], travel)
    got = sweep(
        1, small, {"factor_t": factor_t, "summed": summed, **weights},
        {"phi_out": packed, "factor_out": factor_out, "sound_out": sound_out,
         "den_out": shape((8, rank))},
    )
    den = got["den_out"]
    for iteration in range(2, ITERS):
        got = sweep(
            iteration, small,
            {"factor": got["factor_out"], "summed": sum_over(got["phi_out"], travel),
             "den": den, "sound": got["sound_out"], **weights},
            {"phi_out": packed, "factor_out": factor_out, "sound_out": sound_out},
        )
    out, sound = pl.pallas_call(
        last_kernel,
        in_specs=[pl.BlockSpec(memory_space=pltpu.VMEM)] * 4,
        out_specs=[pl.BlockSpec(memory_space=m) for m in (pltpu.VMEM, pltpu.SMEM)],
        out_shape=[shape((rank, users)), shape((1,), jnp.int32)],
        compiler_params=pltpu.CompilerParams(vmem_limit_bytes=4 * 1024 * 1024),
    )(got["factor_out"], sum_over(got["phi_out"], travel), den, got["sound_out"])
    return out.T, sound.reshape(())


def per_device(mesh, axes, *arrays):
    out, sound = updates(False, mesh, axes, *arrays)
    return lax.cond(sound, lambda *_: out, lambda *a: updates(True, mesh, axes, *a)[0], *arrays)


def solution(mesh):
    axes = tuple(zip(mesh.axis_names, mesh.devices.shape))
    placed = (P(None, "week", "item"), P(), P("item", None), P("week", None))
    run = functools.partial(per_device, mesh, axes)
    return jax.shard_map(run, mesh=mesh, in_specs=placed, out_specs=P(), check_vma=False)
```

```python
import functools

import jax
import jax.numpy as jnp
from jax import lax
from jax.experimental import pallas as pl
from jax.experimental.pallas import tpu as pltpu
from jax.sharding import PartitionSpec as P

ITERS = 3
TILE_USERS = 16
FETCH_USERS = 8
SLOTS = 6
LAG = 2
COLUMNS = 256
GROUP = 4
MOST = 7.0
ROUNDING = 2.8e-6
ALLOWED = 6.4e-9
F32, BF16 = jnp.float32, jnp.bfloat16


def split(x):
    high = x.astype(BF16)
    low = (x - high.astype(F32)).astype(BF16)
    return high, low


def add(parts):
    while len(parts) > 1:
        parts = [p + q for p, q in zip(parts[0::2], parts[1::2])]
    return parts[0]


def sum_over(x, axes):
    for axis, size in axes:
        if size & (size - 1):
            x = lax.psum(x, axis)
            continue
        if size <= GROUP:
            sent = jnp.broadcast_to(x[None], (size, *x.shape))
            parts = lax.all_to_all(sent, axis, 0, 0)
            x = add([parts[k] for k in range(size)])
            continue
        left = size
        while left > 1:
            width = min(GROUP, left)
            left //= width
            parts = [x]
            for k in range(1, width):
                partners = [(i, i ^ (k * left)) for i in range(size)]
                parts.append(lax.ppermute(x, axis, partners))
            x = add(parts)
    return x


def spread(index, multiplier):
    return jnp.exp2(((index * multiplier) & 65535).astype(F32) * (1.0 / 65536.0))


def pack(x):
    half = x.shape[0] // 2
    return jnp.concatenate([x[:half], x[half:]], axis=1)


def unpack(x):
    rank = x.shape[1] // 2
    return jnp.concatenate([x[:, :rank], x[:, rank:]], axis=0)


def column_sums(item_t, week, n_item, n_week):
    rank = item_t.shape[0]
    sums = jnp.broadcast_to(jnp.sum(item_t, axis=1, keepdims=True), (rank, 128)).T[:8]
    sums = sums * (1.0 / n_week)
    weeks = jnp.broadcast_to(jnp.sum(week, axis=0, keepdims=True), sums.shape) * (1.0 / n_item)
    return jnp.concatenate([sums, weeks], axis=1)


def update(factor, phi, den):
    new = factor * phi / den
    spread_sum = jnp.sum(jnp.sum(new / den, axis=0, keepdims=True), axis=1, keepdims=True)
    square_sum = jnp.sum(jnp.sum(new * new, axis=0, keepdims=True), axis=1, keepdims=True)
    sound = jnp.where((MOST * ROUNDING) * spread_sum <= ALLOWED * square_sum, 1.0, 0.0)
    return new, jnp.broadcast_to(sound, (8, 128))


def sweep_kernel(iteration, exact, axes, names, units, *refs):
    r = dict(zip(names, refs))
    counts = r["counts"]
    users, weeks, items = counts.shape
    first = iteration == 0
    rank = r["week"].shape[1]
    rows = TILE_USERS * weeks
    blocks = users // TILE_USERS
    halves = TILE_USERS // FETCH_USERS
    model_w, phi_w, factor_s, week_s = r["model_w"], r["phi_w"], r["factor_s"], r["week_s"]

    def fetch(part):
        at = pl.ds(pl.multiple_of(part * FETCH_USERS, FETCH_USERS), FETCH_USERS)
        slot = lax.rem(part, SLOTS)
        return pltpu.make_async_copy(
            counts.at[at], r["slots"].at[slot], r["arrived"].at[slot]
        )

    week_at = lax.broadcasted_iota(jnp.int32, (weeks, 1), 0) + lax.axis_index("week") * weeks
    week_s[...] = r["week"][...] * spread(week_at, 27146)

    if first:
        for part in range(min(SLOTS, users // FETCH_USERS)):
            fetch(jnp.int32(part)).start()
        item_at = lax.broadcasted_iota(jnp.int32, (1, items), 1)
        item_at = item_at + lax.axis_index("item") * items
        high, low = split(r["item_t"][...] * spread(item_at, 40503))
        model_w[...] = jnp.concatenate([high, high, low, low], axis=0)
        phi_w[:, : 2 * rank] = jnp.concatenate(
            [high.astype(F32), low.astype(F32)], axis=0
        ).T.astype(BF16)
        phi_w[:, 2 * rank:] = jnp.zeros((items, COLUMNS - 2 * rank), BF16)
        factor_s[...] = r["factor_t"][...].T
    else:
        summed = r["summed"][...]
        if iteration == 1:
            sums = summed[users // 2:]
            den = sums[:, :rank] * sums[:, rank:]
            r["den_out"][...] = den
            old = r["factor_t"][...].T
        else:
            den = r["den"][...]
            old = r["factor"][...]
        new, sound = update(old, unpack(summed[: users // 2]), den[0:1, :])
        factor_s[...] = new
        r["factor_out"][...] = new
        r["sound_out"][...] = sound if iteration == 1 else sound * r["sound"][...]

    strips = [slice(n * weeks, (n + 1) * weeks) for n in range(TILE_USERS)]
    chunks = items // COLUMNS
    lhs_s, phi_s = r["lhs_s"], r["phi_s"]

    def operand(user):
        high, low = split(factor_s[pl.ds(user, 1), :] * week_s[...])
        return jnp.concatenate([high, low, high, low], axis=1)

    def push_model(chunk):
        at = pl.ds(chunk % chunks * COLUMNS, COLUMNS)
        pltpu.matmul_push_rhs(model_w[:, at], 0, 0)

    def push_phi(chunk):
        at = pl.ds(chunk % chunks * COLUMNS, COLUMNS)
        pltpu.matmul_push_rhs(phi_w[at, :], 0, 1)

    def matmuls(ahead, total):
        def keep(n, user):
            sums = pltpu.matmul_pop(total[n])
            sums = (sums[:, :rank] + sums[:, rank: 2 * rank]) * week_s[...]
            phi_s[pl.ds(user, 1), :] = jnp.sum(sums, axis=0, keepdims=True)

        push_model(0)
        for n, strip in enumerate(strips):
            lhs_s[strip, :] = operand(n)
            pltpu.matmul_acc_lhs(ahead[n], lhs_s[strip, :], None if n else 0)
        push_model(1)
        push_phi(0)

        def body(block, carry):
            start = block * TILE_USERS
            before = lax.rem(start + users - TILE_USERS, users)
            after = jnp.minimum(start + TILE_USERS, users - TILE_USERS)
            lagging = []

            def add_phi():
                chunk, n, parts = lagging.pop(0)
                if chunk == 0:
                    keep(n, before + n)
                pltpu.matmul_acc_lhs(total[n], parts[0], None if n else 0)
                for part in parts[1:]:
                    pltpu.matmul_acc_lhs(total[n], part)
                if n == len(strips) // 2:
                    push_phi(chunk + 1)

            for chunk in range(chunks):
                at = slice(chunk * COLUMNS, (chunk + 1) * COLUMNS)
                for n, strip in enumerate(strips):
                    part = block * halves + n // FETCH_USERS
                    if first and chunk == 0 and n % FETCH_USERS == 0:
                        fetch(part).wait()
                    model = pltpu.matmul_pop(ahead[n])
                    if chunk + 1 < chunks:
                        lhs = lhs_s[strip, :]
                    else:
                        lhs = operand(after + n)
                        lhs_s[strip, :] = lhs
                    pltpu.matmul_acc_lhs(ahead[n], lhs, None if n else 0)
                    if n == len(strips) // 2:
                        push_model(chunk + 2)
                    if first:
                        count = r["slots"][lax.rem(part, SLOTS), n % FETCH_USERS, :, at]
                        r["small_out"][start + n, :, at] = count.astype(jnp.int8)
                    else:
                        count = counts[start + n, :, at].astype(jnp.int32)
                    ratio = count.astype(F32) * pltpu.reciprocal(
                        model, approx=True, full_range=False
                    )
                    lagging.append((chunk, n, split(ratio) if exact else (ratio.astype(BF16),)))
                    if len(lagging) > LAG:
                        add_phi()
            while lagging:
                add_phi()
            if first:

                @pl.when((block + 1) * halves + SLOTS <= users // FETCH_USERS)
                def _():
                    for half in range(halves):
                        fetch(block * halves + SLOTS + half).start()

            return carry

        lax.fori_loop(0, blocks, body, 0)
        for n in range(TILE_USERS):
            keep(n, users - TILE_USERS + n)
        nothing = jnp.zeros((weeks, COLUMNS), BF16)
        for ref in ahead:
            pltpu.matmul_pop(ref)
        for ref in (ahead[0], total[0]):
            pltpu.matmul_acc_lhs(ref, nothing, 0)
            pltpu.matmul_pop(ref)

    pl.run_scoped(matmuls, *[[unit] * TILE_USERS for unit in units])
    r["phi_out"][: users // 2, :] = pack(phi_s[...])
    if first:
        n_item, n_week = (dict(axes)[a] for a in ("item", "week"))
        r["phi_out"][users // 2:, :] = column_sums(r["item_t"][...], r["week"][...], n_item, n_week)


def last_kernel(factor, summed, den, sound, out, sound_out):
    new, fine = update(factor[...], unpack(summed[...]), den[0:1, :])
    out[...] = new.T
    sound_out[0] = jnp.min(fine * sound[...]).astype(jnp.int32)


def updates(exact, mesh, axes, counts, user_factor, item_factor, week_factor):
    users, rank = user_factor.shape
    weeks, items = counts.shape[1:]
    rows = TILE_USERS * weeks
    factor_t, item_t = user_factor.T, item_factor.T
    travel = sorted(axes, reverse=True)

    def shape(dims, dtype=F32):
        return jax.ShapeDtypeStruct(dims, dtype)

    stream = {
        "slots": pltpu.VMEM((SLOTS, FETCH_USERS, weeks, items), jnp.int32),
        "arrived": pltpu.SemaphoreType.DMA((SLOTS,)),
    }
    scratch = {
        "factor_s": pltpu.VMEM((users, rank), F32),
        "week_s": pltpu.VMEM((weeks, rank), F32),
        "phi_s": pltpu.VMEM((users, rank), F32),
        "lhs_s": pltpu.VMEM((rows, 4 * rank), BF16),
    }
    with jax.sharding.use_abstract_mesh(mesh.abstract_mesh):
        units = [pltpu.ACC(unit)((weeks, COLUMNS), F32) for unit in (0, 1)]

    def sweep(iteration, counts, ins, outs):
        ins = {"counts": counts, "week": week_factor, **ins}
        first = iteration == 0
        scratches = {**stream, **scratch} if first else scratch
        names = list(ins) + list(outs) + list(scratches)
        results = pl.pallas_call(
            functools.partial(sweep_kernel, iteration, exact, axes, names, units),
            in_specs=[
                pl.BlockSpec(memory_space=pl.ANY if first and n == "counts" else pltpu.VMEM)
                for n in ins
            ],
            out_specs=[pl.BlockSpec(memory_space=pltpu.VMEM)] * len(outs),
            out_shape=list(outs.values()),
            scratch_shapes=list(scratches.values()),
            compiler_params=pltpu.CompilerParams(vmem_limit_bytes=(28 if first else 8) * 1024 * 1024),
            cost_estimate=pl.CostEstimate(
                flops=2 * (3 if exact else 2) * users * weeks * items * 256,
                bytes_accessed=4 * users * weeks * items,
                transcendentals=0,
            ),
        )(*ins.values())
        return dict(zip(outs, results))

    packed = shape((users // 2, 2 * rank))
    factor_out, sound_out = shape((users, rank)), shape((8, 128))
    got = sweep(
        0, counts, {"factor_t": factor_t, "item_t": item_t},
        {"phi_out": shape((users // 2 + 8, 2 * rank)), "small_out": shape(counts.shape, jnp.int8),
         "model_w": shape((4 * rank, items), BF16), "phi_w": shape((items, COLUMNS), BF16)},
    )
    small, weights = got["small_out"], {n: got[n] for n in ("model_w", "phi_w")}
    summed = sum_over(got["phi_out"], travel)
    got = sweep(
        1, small, {"factor_t": factor_t, "summed": summed, **weights},
        {"phi_out": packed, "factor_out": factor_out, "sound_out": sound_out,
         "den_out": shape((8, rank))},
    )
    den = got["den_out"]
    for iteration in range(2, ITERS):
        got = sweep(
            iteration, small,
            {"factor": got["factor_out"], "summed": sum_over(got["phi_out"], travel),
             "den": den, "sound": got["sound_out"], **weights},
            {"phi_out": packed, "factor_out": factor_out, "sound_out": sound_out},
        )
    out, sound = pl.pallas_call(
        last_kernel,
        in_specs=[pl.BlockSpec(memory_space=pltpu.VMEM)] * 4,
        out_specs=[pl.BlockSpec(memory_space=m) for m in (pltpu.VMEM, pltpu.SMEM)],
        out_shape=[shape((rank, users)), shape((1,), jnp.int32)],
        compiler_params=pltpu.CompilerParams(vmem_limit_bytes=4 * 1024 * 1024),
    )(got["factor_out"], sum_over(got["phi_out"], travel), den, got["sound_out"])
    return out.T, sound.reshape(())


def per_device(mesh, axes, *arrays):
    out, sound = updates(False, mesh, axes, *arrays)
    return lax.cond(sound, lambda *_: out, lambda *a: updates(True, mesh, axes, *a)[0], *arrays)


def solution(mesh):
    axes = tuple(zip(mesh.axis_names, mesh.devices.shape))
    placed = (P(None, "week", "item"), P(), P("item", None), P("week", None))
    run = functools.partial(per_device, mesh, axes)
    return jax.shard_map(run, mesh=mesh, in_specs=placed, out_specs=P(), check_vma=False)
```

```python
import functools

import jax
import jax.numpy as jnp
from jax import lax
from jax.experimental import pallas as pl
from jax.experimental.pallas import tpu as pltpu
from jax.sharding import PartitionSpec as P

ITERS = 3
FIRST_TILE, NEXT_TILE = 8, 16
SLOTS = 4
LAG = 2
COLUMNS = 256
GROUP = 4
MOST = 7.0
ROUNDING = 5.6e-6
ALLOWED = 6.4e-9
F32, BF16 = jnp.float32, jnp.bfloat16
SMALL = jnp.float8_e4m3fn


def split(x):
    high = x.astype(BF16)
    low = (x - high.astype(F32)).astype(BF16)
    return high, low


def add(parts):
    while len(parts) > 1:
        parts = [p + q for p, q in zip(parts[0::2], parts[1::2])]
    return parts[0]


def sum_over(x, axes):
    for axis, size in axes:
        if size & (size - 1):
            x = lax.psum(x, axis)
            continue
        left = size
        while left > 1:
            width = min(GROUP, left)
            left //= width
            parts = [x]
            for k in range(1, width):
                partners = [(i, i ^ (k * left)) for i in range(size)]
                parts.append(lax.ppermute(x, axis, partners))
            x = add(parts)
    return x


def spread(index, multiplier):
    return jnp.exp2(((index * multiplier) & 65535).astype(F32) * (1.0 / 65536.0))


def pack(x):
    half = x.shape[0] // 2
    return jnp.concatenate([x[:half], x[half:]], axis=1)


def unpack(x):
    rank = x.shape[1] // 2
    return jnp.concatenate([x[:, :rank], x[:, rank:]], axis=0)


def column_sums(item_t, week, n_item, n_week):
    rank = item_t.shape[0]
    sums = jnp.broadcast_to(jnp.sum(item_t, axis=1, keepdims=True), (rank, 128)).T[:8]
    sums = sums * (1.0 / n_week)
    weeks = jnp.broadcast_to(jnp.sum(week, axis=0, keepdims=True), sums.shape) * (1.0 / n_item)
    return jnp.concatenate([sums, weeks], axis=1)


def update(factor, phi, den):
    new = factor * phi / den
    spread_sum = jnp.sum(jnp.sum(new / den, axis=0, keepdims=True), axis=1, keepdims=True)
    square_sum = jnp.sum(jnp.sum(new * new, axis=0, keepdims=True), axis=1, keepdims=True)
    sound = jnp.where((MOST * ROUNDING) * spread_sum <= ALLOWED * square_sum, 1.0, 0.0)
    return new, jnp.broadcast_to(sound, (8, 128))


def sweep_kernel(iteration, exact, axes, names, units, *refs):
    r = dict(zip(names, refs))
    counts = r["counts"]
    users, weeks, items = counts.shape
    first = iteration == 0
    stream = "slots" in r
    rank = r["week"].shape[1]
    tile = FIRST_TILE if stream else NEXT_TILE
    blocks = users // tile
    model_w, phi_w, factor_s, week_s = r["model_w"], r["phi_w"], r["factor_s"], r["week_s"]

    def fetch(block):
        at = pl.ds(pl.multiple_of(block * tile, tile), tile)
        slot = lax.rem(block, SLOTS)
        return pltpu.make_async_copy(
            counts.at[at], r["slots"].at[slot], r["arrived"].at[slot]
        )

    week_at = lax.broadcasted_iota(jnp.int32, (weeks, 1), 0) + lax.axis_index("week") * weeks
    week_s[...] = r["week"][...] * spread(week_at, 27146)

    if stream:
        for block in range(min(SLOTS, blocks)):
            fetch(jnp.int32(block)).start()
    if first:
        item_at = lax.broadcasted_iota(jnp.int32, (1, items), 1)
        item_at = item_at + lax.axis_index("item") * items
        high, low = split(r["item_t"][...] * spread(item_at, 40503))
        model_w[...] = jnp.concatenate([high, high, low, low], axis=0)
        phi_w[:, : 2 * rank] = jnp.concatenate(
            [high.astype(F32), low.astype(F32)], axis=0
        ).T.astype(BF16)
        phi_w[:, 2 * rank:] = jnp.zeros((items, COLUMNS - 2 * rank), BF16)
        factor_s[...] = r["factor_t"][...].T
    else:
        summed = r["summed"][...]
        if iteration == 1:
            sums = summed[users // 2:]
            den = sums[:, :rank] * sums[:, rank:]
            r["den_out"][...] = den
            old = r["factor_t"][...].T
        else:
            den = r["den"][...]
            old = r["factor"][...]
        new, sound = update(old, unpack(summed[: users // 2]), den[0:1, :])
        factor_s[...] = new
        r["factor_out"][...] = new
        r["sound_out"][...] = sound if iteration == 1 else sound * r["sound"][...]

    strips = [slice(n * weeks, (n + 1) * weeks) for n in range(tile)]
    chunks = items // COLUMNS
    lhs_s, phi_s = r["lhs_s"], r["phi_s"]

    def operand(user):
        high, low = split(factor_s[pl.ds(user, 1), :] * week_s[...])
        return jnp.concatenate([high, low, high, low], axis=1)

    def push_model(chunk):
        at = pl.ds(chunk % chunks * COLUMNS, COLUMNS)
        pltpu.matmul_push_rhs(model_w[:, at], 0, 0)

    def push_phi(chunk):
        at = pl.ds(chunk % chunks * COLUMNS, COLUMNS)
        pltpu.matmul_push_rhs(phi_w[at, :], 0, 1)

    def matmuls(ahead, total):
        def keep(n, user):
            sums = pltpu.matmul_pop(total[n])
            sums = (sums[:, :rank] + sums[:, rank: 2 * rank]) * week_s[...]
            phi_s[pl.ds(user, 1), :] = jnp.sum(sums, axis=0, keepdims=True)

        push_model(0)
        for n, strip in enumerate(strips):
            lhs_s[strip, :] = operand(n)
            pltpu.matmul_acc_lhs(ahead[n], lhs_s[strip, :], None if n else 0)
        push_model(1)
        push_phi(0)

        def body(block, carry):
            start = block * tile
            before = lax.rem(start + users - tile, users)
            after = jnp.minimum(start + tile, users - tile)
            lagging = []
            if stream:
                fetch(block).wait()

            def add_phi():
                chunk, n, parts = lagging.pop(0)
                if chunk == 0:
                    keep(n, before + n)
                pltpu.matmul_acc_lhs(total[n], parts[0], None if n else 0)
                for part in parts[1:]:
                    pltpu.matmul_acc_lhs(total[n], part)
                if n == len(strips) // 2:
                    push_phi(chunk + 1)

            for chunk in range(chunks):
                at = slice(chunk * COLUMNS, (chunk + 1) * COLUMNS)
                for n, strip in enumerate(strips):
                    model = pltpu.matmul_pop(ahead[n])
                    if chunk + 1 < chunks:
                        lhs = lhs_s[strip, :]
                    else:
                        lhs = operand(after + n)
                        lhs_s[strip, :] = lhs
                    pltpu.matmul_acc_lhs(ahead[n], lhs, None if n else 0)
                    if n == len(strips) // 2:
                        push_model(chunk + 2)
                    if stream:
                        count = r["slots"][lax.rem(block, SLOTS), n, :, at]
                        count = count.astype(F32)
                        if "small_out" in r:
                            r["small_out"][start + n, :, at] = count.astype(SMALL)
                        count = count.astype(BF16)
                    else:
                        count = counts[start + n, :, at].astype(BF16)
                    inverse = pltpu.reciprocal(model, approx=True, full_range=False)
                    if exact:
                        parts = split(count.astype(F32) * inverse)
                    else:
                        parts = (count * inverse.astype(BF16),)
                    lagging.append((chunk, n, parts))
                    if len(lagging) > LAG:
                        add_phi()
            while lagging:
                add_phi()
            if stream:

                @pl.when(block + SLOTS < blocks)
                def _():
                    fetch(block + SLOTS).start()

            return carry

        lax.fori_loop(0, blocks, body, 0)
        for n in range(tile):
            keep(n, users - tile + n)
        nothing = jnp.zeros((weeks, COLUMNS), BF16)
        for ref in ahead:
            pltpu.matmul_pop(ref)
        for ref in (ahead[0], total[0]):
            pltpu.matmul_acc_lhs(ref, nothing, 0)
            pltpu.matmul_pop(ref)

    pl.run_scoped(matmuls, *[[unit] * tile for unit in units])
    r["phi_out"][: users // 2, :] = pack(phi_s[...])
    if first:
        n_item, n_week = (dict(axes)[a] for a in ("item", "week"))
        r["phi_out"][users // 2:, :] = column_sums(r["item_t"][...], r["week"][...], n_item, n_week)


def last_kernel(factor, summed, den, sound, out, sound_out):
    new, fine = update(factor[...], unpack(summed[...]), den[0:1, :])
    out[...] = new.T
    sound_out[0] = jnp.min(fine * sound[...]).astype(jnp.int32)


def updates(exact, mesh, axes, counts, user_factor, item_factor, week_factor):
    users, rank = user_factor.shape
    weeks, items = counts.shape[1:]
    factor_t, item_t = user_factor.T, item_factor.T
    travel = sorted(axes, reverse=True)

    def shape(dims, dtype=F32):
        return jax.ShapeDtypeStruct(dims, dtype)

    stream = {
        "slots": pltpu.VMEM((SLOTS, FIRST_TILE, weeks, items), jnp.int32),
        "arrived": pltpu.SemaphoreType.DMA((SLOTS,)),
    }
    scratch = {
        "factor_s": pltpu.VMEM((users, rank), F32),
        "week_s": pltpu.VMEM((weeks, rank), F32),
        "phi_s": pltpu.VMEM((users, rank), F32),
        "lhs_s": pltpu.VMEM((NEXT_TILE * weeks, 4 * rank), BF16),
    }
    with jax.sharding.use_abstract_mesh(mesh.abstract_mesh):
        units = [pltpu.ACC(unit)((weeks, COLUMNS), F32) for unit in (0, 1)]

    def sweep(iteration, counts, ins, outs):
        ins = {"counts": counts, "week": week_factor, **ins}
        streamed = counts.dtype == jnp.int32
        scratches = {**stream, **scratch} if streamed else scratch
        names = list(ins) + list(outs) + list(scratches)
        results = pl.pallas_call(
            functools.partial(sweep_kernel, iteration, exact, axes, names, units),
            in_specs=[
                pl.BlockSpec(memory_space=pl.ANY if streamed and n == "counts" else pltpu.VMEM)
                for n in ins
            ],
            out_specs=[pl.BlockSpec(memory_space=pltpu.VMEM)] * len(outs),
            out_shape=list(outs.values()),
            scratch_shapes=list(scratches.values()),
            compiler_params=pltpu.CompilerParams(vmem_limit_bytes=(22 if streamed else 8) * 1024 * 1024),
            cost_estimate=pl.CostEstimate(
                flops=2 * (3 if exact else 2) * users * weeks * items * 256,
                bytes_accessed=4 * users * weeks * items,
                transcendentals=0,
            ),
        )(*ins.values())
        return dict(zip(outs, results))

    packed = shape((users // 2, 2 * rank))
    factor_out, sound_out = shape((users, rank)), shape((8, 128))
    outs = {
        "phi_out": shape((users // 2 + 8, 2 * rank)),
        "model_w": shape((4 * rank, items), BF16),
        "phi_w": shape((items, COLUMNS), BF16),
    }
    if not exact:
        outs["small_out"] = shape(counts.shape, SMALL)
    got = sweep(0, counts, {"factor_t": factor_t, "item_t": item_t}, outs)
    small, weights = got.get("small_out", counts), {n: got[n] for n in ("model_w", "phi_w")}
    summed = sum_over(got["phi_out"], travel)
    got = sweep(
        1, small, {"factor_t": factor_t, "summed": summed, **weights},
        {"phi_out": packed, "factor_out": factor_out, "sound_out": sound_out,
         "den_out": shape((8, rank))},
    )
    den = got["den_out"]
    for iteration in range(2, ITERS):
        got = sweep(
            iteration, small,
            {"factor": got["factor_out"], "summed": sum_over(got["phi_out"], travel),
             "den": den, "sound": got["sound_out"], **weights},
            {"phi_out": packed, "factor_out": factor_out, "sound_out": sound_out},
        )
    out, sound = pl.pallas_call(
        last_kernel,
        in_specs=[pl.BlockSpec(memory_space=pltpu.VMEM)] * 4,
        out_specs=[pl.BlockSpec(memory_space=m) for m in (pltpu.VMEM, pltpu.SMEM)],
        out_shape=[shape((rank, users)), shape((1,), jnp.int32)],
        compiler_params=pltpu.CompilerParams(vmem_limit_bytes=4 * 1024 * 1024),
    )(got["factor_out"], sum_over(got["phi_out"], travel), den, got["sound_out"])
    return out.T, sound.reshape(())


def per_device(mesh, axes, *arrays):
    out, sound = updates(False, mesh, axes, *arrays)
    return lax.cond(sound, lambda *_: out, lambda *a: updates(True, mesh, axes, *a)[0], *arrays)


def solution(mesh):
    axes = tuple(zip(mesh.axis_names, mesh.devices.shape))
    placed = (P(None, "week", "item"), P(), P("item", None), P("week", None))
    run = functools.partial(per_device, mesh, axes)
    return jax.shard_map(run, mesh=mesh, in_specs=placed, out_specs=P(), check_vma=False)
```

```python
import functools

import jax
import jax.numpy as jnp
from jax import lax
from jax.experimental import pallas as pl
from jax.experimental.pallas import tpu as pltpu
from jax.sharding import PartitionSpec as P

ITERS = 3
FIRST_TILE, NEXT_TILE = 8, 16
SLOTS = 4
LAG = 2
COLUMNS = 256
GROUP = 4
MOST = 7.0
ROUNDING = 9.2e-6
ALLOWED = 6.4e-9
F32, BF16 = jnp.float32, jnp.bfloat16
SMALL = jnp.float8_e4m3fn


def split(x):
    high = x.astype(BF16)
    low = (x - high.astype(F32)).astype(BF16)
    return high, low


def add(parts):
    while len(parts) > 1:
        parts = [p + q for p, q in zip(parts[0::2], parts[1::2])]
    return parts[0]


def sum_over(x, axes):
    for axis, size in axes:
        if size & (size - 1):
            x = lax.psum(x, axis)
            continue
        left = size
        while left > 1:
            width = min(GROUP, left)
            left //= width
            parts = [x]
            for k in range(1, width):
                partners = [(i, i ^ (k * left)) for i in range(size)]
                parts.append(lax.ppermute(x, axis, partners))
            x = add(parts)
    return x


def spread(index, multiplier):
    return jnp.exp2(((index * multiplier) & 65535).astype(F32) * (1.0 / 65536.0))


def pack(x):
    half = x.shape[0] // 2
    return jnp.concatenate([x[:half], x[half:]], axis=1)


def unpack(x):
    rank = x.shape[1] // 2
    return jnp.concatenate([x[:, :rank], x[:, rank:]], axis=0)


def column_sums(item_t, week, n_item, n_week):
    rank = item_t.shape[0]
    sums = jnp.broadcast_to(jnp.sum(item_t, axis=1, keepdims=True), (rank, 128)).T[:8]
    sums = sums * (1.0 / n_week)
    weeks = jnp.broadcast_to(jnp.sum(week, axis=0, keepdims=True), sums.shape) * (1.0 / n_item)
    return jnp.concatenate([sums, weeks], axis=1)


def update(factor, phi, den):
    new = factor * phi / den
    spread_sum = jnp.sum(jnp.sum(new / den, axis=0, keepdims=True), axis=1, keepdims=True)
    square_sum = jnp.sum(jnp.sum(new * new, axis=0, keepdims=True), axis=1, keepdims=True)
    sound = jnp.where((MOST * ROUNDING) * spread_sum <= ALLOWED * square_sum, 1.0, 0.0)
    return new, jnp.broadcast_to(sound, (8, 128))


def sweep_kernel(iteration, exact, axes, names, units, *refs):
    r = dict(zip(names, refs))
    counts = r["counts"]
    users, weeks, items = counts.shape
    first = iteration == 0
    stream = "slots" in r
    rank = r["week"].shape[1]
    tile = FIRST_TILE if stream else NEXT_TILE
    blocks = users // tile
    model_w, phi_w, factor_s, week_s = r["model_w"], r["phi_w"], r["factor_s"], r["week_s"]

    def fetch(block):
        at = pl.ds(pl.multiple_of(block * tile, tile), tile)
        slot = lax.rem(block, SLOTS)
        return pltpu.make_async_copy(
            counts.at[at], r["slots"].at[slot], r["arrived"].at[slot]
        )

    week_at = lax.broadcasted_iota(jnp.int32, (weeks, 1), 0) + lax.axis_index("week") * weeks
    week_s[...] = r["week"][...] * spread(week_at, 27146)

    if stream:
        for block in range(min(SLOTS, blocks)):
            fetch(jnp.int32(block)).start()
    if first:
        item_at = lax.broadcasted_iota(jnp.int32, (1, items), 1)
        item_at = item_at + lax.axis_index("item") * items
        high, low = split(r["item_t"][...] * spread(item_at, 40503))
        model_w[...] = jnp.concatenate([high, high, low, low], axis=0)
        phi_w[:, : 2 * rank] = jnp.concatenate(
            [high.astype(F32), low.astype(F32)], axis=0
        ).T.astype(BF16)
        phi_w[:, 2 * rank:] = jnp.zeros((items, COLUMNS - 2 * rank), BF16)
        factor_s[...] = r["factor_t"][...].T
    else:
        summed = r["summed"][...]
        if iteration == 1:
            sums = summed[users // 2:]
            den = sums[:, :rank] * sums[:, rank:]
            r["den_out"][...] = den
            old = r["factor_t"][...].T
        else:
            den = r["den"][...]
            old = r["factor"][...]
        new, sound = update(old, unpack(summed[: users // 2]), den[0:1, :])
        factor_s[...] = new
        r["factor_out"][...] = new
        r["sound_out"][...] = sound if iteration == 1 else sound * r["sound"][...]

    strips = [slice(n * weeks, (n + 1) * weeks) for n in range(tile)]
    chunks = items // COLUMNS
    lhs_s, phi_s = r["lhs_s"], r["phi_s"]

    def operand(user):
        high, low = split(factor_s[pl.ds(user, 1), :] * week_s[...])
        return jnp.concatenate([high, low, high, low], axis=1)

    def push_model(chunk):
        at = pl.ds(chunk % chunks * COLUMNS, COLUMNS)
        pltpu.matmul_push_rhs(model_w[:, at], 0, 0)

    def push_phi(chunk):
        at = pl.ds(chunk % chunks * COLUMNS, COLUMNS)
        pltpu.matmul_push_rhs(phi_w[at, :], 0, 1)

    def matmuls(ahead, total):
        def keep(n, user):
            sums = pltpu.matmul_pop(total[n])
            sums = (sums[:, :rank] + sums[:, rank: 2 * rank]) * week_s[...]
            phi_s[pl.ds(user, 1), :] = jnp.sum(sums, axis=0, keepdims=True)

        push_model(0)
        for n, strip in enumerate(strips):
            lhs_s[strip, :] = operand(n)
            pltpu.matmul_acc_lhs(ahead[n], lhs_s[strip, :], None if n else 0)
        push_model(1)
        push_phi(0)

        def body(block, carry):
            start = block * tile
            before = lax.rem(start + users - tile, users)
            after = jnp.minimum(start + tile, users - tile)
            lagging = []
            if stream:
                fetch(block).wait()

            def add_phi():
                chunk, n, parts = lagging.pop(0)
                if chunk == 0:
                    keep(n, before + n)
                pltpu.matmul_acc_lhs(total[n], parts[0], None if n else 0)
                for part in parts[1:]:
                    pltpu.matmul_acc_lhs(total[n], part)
                if n == len(strips) // 2:
                    push_phi(chunk + 1)

            for chunk in range(chunks):
                at = slice(chunk * COLUMNS, (chunk + 1) * COLUMNS)
                for n, strip in enumerate(strips):
                    model = pltpu.matmul_pop(ahead[n])
                    if chunk + 1 < chunks:
                        lhs = lhs_s[strip, :]
                    else:
                        lhs = operand(after + n)
                        lhs_s[strip, :] = lhs
                    pltpu.matmul_acc_lhs(ahead[n], lhs, None if n else 0)
                    if n == len(strips) // 2:
                        push_model(chunk + 2)
                    if stream:
                        count = r["slots"][lax.rem(block, SLOTS), n, :, at]
                        count = count.astype(F32)
                        if "small_out" in r:
                            r["small_out"][start + n, :, at] = count.astype(SMALL)
                        count = count.astype(BF16)
                    else:
                        count = counts[start + n, :, at].astype(BF16)
                    if not exact:
                        model = model.astype(BF16)
                    inverse = pltpu.reciprocal(model, approx=True, full_range=False)
                    if exact:
                        parts = split(count.astype(F32) * inverse)
                    else:
                        parts = (count * inverse,)
                    lagging.append((chunk, n, parts))
                    if len(lagging) > LAG:
                        add_phi()
            while lagging:
                add_phi()
            if stream:

                @pl.when(block + SLOTS < blocks)
                def _():
                    fetch(block + SLOTS).start()

            return carry

        lax.fori_loop(0, blocks, body, 0)
        for n in range(tile):
            keep(n, users - tile + n)
        nothing = jnp.zeros((weeks, COLUMNS), BF16)
        for ref in ahead:
            pltpu.matmul_pop(ref)
        for ref in (ahead[0], total[0]):
            pltpu.matmul_acc_lhs(ref, nothing, 0)
            pltpu.matmul_pop(ref)

    pl.run_scoped(matmuls, *[[unit] * tile for unit in units])
    r["phi_out"][: users // 2, :] = pack(phi_s[...])
    if first:
        n_item, n_week = (dict(axes)[a] for a in ("item", "week"))
        r["phi_out"][users // 2:, :] = column_sums(r["item_t"][...], r["week"][...], n_item, n_week)


def last_kernel(factor, summed, den, sound, out, sound_out):
    new, fine = update(factor[...], unpack(summed[...]), den[0:1, :])
    out[...] = new.T
    sound_out[0] = jnp.min(fine * sound[...]).astype(jnp.int32)


def updates(exact, mesh, axes, counts, user_factor, item_factor, week_factor):
    users, rank = user_factor.shape
    weeks, items = counts.shape[1:]
    factor_t, item_t = user_factor.T, item_factor.T
    travel = sorted(axes, reverse=True)

    def shape(dims, dtype=F32):
        return jax.ShapeDtypeStruct(dims, dtype)

    stream = {
        "slots": pltpu.VMEM((SLOTS, FIRST_TILE, weeks, items), jnp.int32),
        "arrived": pltpu.SemaphoreType.DMA((SLOTS,)),
    }
    scratch = {
        "factor_s": pltpu.VMEM((users, rank), F32),
        "week_s": pltpu.VMEM((weeks, rank), F32),
        "phi_s": pltpu.VMEM((users, rank), F32),
        "lhs_s": pltpu.VMEM((NEXT_TILE * weeks, 4 * rank), BF16),
    }
    with jax.sharding.use_abstract_mesh(mesh.abstract_mesh):
        units = [pltpu.ACC(unit)((weeks, COLUMNS), F32) for unit in (0, 1)]

    def sweep(iteration, counts, ins, outs):
        ins = {"counts": counts, "week": week_factor, **ins}
        streamed = counts.dtype == jnp.int32
        scratches = {**stream, **scratch} if streamed else scratch
        names = list(ins) + list(outs) + list(scratches)
        results = pl.pallas_call(
            functools.partial(sweep_kernel, iteration, exact, axes, names, units),
            in_specs=[
                pl.BlockSpec(memory_space=pl.ANY if streamed and n == "counts" else pltpu.VMEM)
                for n in ins
            ],
            out_specs=[pl.BlockSpec(memory_space=pltpu.VMEM)] * len(outs),
            out_shape=list(outs.values()),
            scratch_shapes=list(scratches.values()),
            compiler_params=pltpu.CompilerParams(vmem_limit_bytes=(22 if streamed else 8) * 1024 * 1024),
            cost_estimate=pl.CostEstimate(
                flops=2 * (3 if exact else 2) * users * weeks * items * 256,
                bytes_accessed=4 * users * weeks * items,
                transcendentals=0,
            ),
        )(*ins.values())
        return dict(zip(outs, results))

    packed = shape((users // 2, 2 * rank))
    factor_out, sound_out = shape((users, rank)), shape((8, 128))
    outs = {
        "phi_out": shape((users // 2 + 8, 2 * rank)),
        "model_w": shape((4 * rank, items), BF16),
        "phi_w": shape((items, COLUMNS), BF16),
    }
    if not exact:
        outs["small_out"] = shape(counts.shape, SMALL)
    got = sweep(0, counts, {"factor_t": factor_t, "item_t": item_t}, outs)
    small, weights = got.get("small_out", counts), {n: got[n] for n in ("model_w", "phi_w")}
    summed = sum_over(got["phi_out"], travel)
    got = sweep(
        1, small, {"factor_t": factor_t, "summed": summed, **weights},
        {"phi_out": packed, "factor_out": factor_out, "sound_out": sound_out,
         "den_out": shape((8, rank))},
    )
    den = got["den_out"]
    for iteration in range(2, ITERS):
        got = sweep(
            iteration, small,
            {"factor": got["factor_out"], "summed": sum_over(got["phi_out"], travel),
             "den": den, "sound": got["sound_out"], **weights},
            {"phi_out": packed, "factor_out": factor_out, "sound_out": sound_out},
        )
    out, sound = pl.pallas_call(
        last_kernel,
        in_specs=[pl.BlockSpec(memory_space=pltpu.VMEM)] * 4,
        out_specs=[pl.BlockSpec(memory_space=m) for m in (pltpu.VMEM, pltpu.SMEM)],
        out_shape=[shape((rank, users)), shape((1,), jnp.int32)],
        compiler_params=pltpu.CompilerParams(vmem_limit_bytes=4 * 1024 * 1024),
    )(got["factor_out"], sum_over(got["phi_out"], travel), den, got["sound_out"])
    return out.T, sound.reshape(())


def per_device(mesh, axes, *arrays):
    out, sound = updates(False, mesh, axes, *arrays)
    return lax.cond(sound, lambda *_: out, lambda *a: updates(True, mesh, axes, *a)[0], *arrays)


def solution(mesh):
    axes = tuple(zip(mesh.axis_names, mesh.devices.shape))
    placed = (P(None, "week", "item"), P(), P("item", None), P("week", None))
    run = functools.partial(per_device, mesh, axes)
    return jax.shard_map(run, mesh=mesh, in_specs=placed, out_specs=P(), check_vma=False)
```

```python
import functools

import jax
import jax.numpy as jnp
from jax import lax
from jax.experimental import pallas as pl
from jax.experimental.pallas import tpu as pltpu
from jax.sharding import PartitionSpec as P

ITERS = 3
FIRST_TILE, NEXT_TILE = 8, 16
SLOTS = 4
LAG = 2
COLUMNS = 256
GROUP = 4
MOST = 7.0
ROUNDING = 5.6e-6
ALLOWED = 6.4e-9
F32, BF16 = jnp.float32, jnp.bfloat16
SMALL = jnp.float8_e4m3fn


def split(x):
    high = x.astype(BF16)
    low = (x - high.astype(F32)).astype(BF16)
    return high, low


def add(parts):
    while len(parts) > 1:
        parts = [p + q for p, q in zip(parts[0::2], parts[1::2])]
    return parts[0]


def sum_over(x, axes):
    for axis, size in axes:
        if size & (size - 1):
            x = lax.psum(x, axis)
            continue
        left = size
        while left > 1:
            width = min(GROUP, left)
            left //= width
            parts = [x]
            for k in range(1, width):
                partners = [(i, i ^ (k * left)) for i in range(size)]
                parts.append(lax.ppermute(x, axis, partners))
            x = add(parts)
    return x


def spread(index, multiplier):
    return jnp.exp2(((index * multiplier) & 65535).astype(F32) * (1.0 / 65536.0))


def pack(x):
    half = x.shape[0] // 2
    return jnp.concatenate([x[:half], x[half:]], axis=1)


def unpack(x):
    rank = x.shape[1] // 2
    return jnp.concatenate([x[:, :rank], x[:, rank:]], axis=0)


def column_sums(item_t, week, n_item, n_week):
    rank = item_t.shape[0]
    sums = jnp.broadcast_to(jnp.sum(item_t, axis=1, keepdims=True), (rank, 128)).T[:8]
    sums = sums * (1.0 / n_week)
    weeks = jnp.broadcast_to(jnp.sum(week, axis=0, keepdims=True), sums.shape) * (1.0 / n_item)
    return jnp.concatenate([sums, weeks], axis=1)


def update(factor, phi, den):
    new = factor * phi / den
    spread_sum = jnp.sum(jnp.sum(new / den, axis=0, keepdims=True), axis=1, keepdims=True)
    square_sum = jnp.sum(jnp.sum(new * new, axis=0, keepdims=True), axis=1, keepdims=True)
    sound = jnp.where((MOST * ROUNDING) * spread_sum <= ALLOWED * square_sum, 1.0, 0.0)
    return new, jnp.broadcast_to(sound, (8, 128))


def sweep_kernel(iteration, exact, axes, names, units, *refs):
    r = dict(zip(names, refs))
    counts = r["counts"]
    users, weeks, items = counts.shape
    first = iteration == 0
    stream = "slots" in r
    rank = r["week"].shape[1]
    tile = FIRST_TILE if stream else NEXT_TILE
    blocks = users // tile
    model_w, phi_w, factor_s, week_s = r["model_w"], r["phi_w"], r["factor_s"], r["week_s"]

    def fetch(block):
        at = pl.ds(pl.multiple_of(block * tile, tile), tile)
        slot = lax.rem(block, SLOTS)
        return pltpu.make_async_copy(
            counts.at[at], r["slots"].at[slot], r["arrived"].at[slot]
        )

    week_at = lax.broadcasted_iota(jnp.int32, (weeks, 1), 0) + lax.axis_index("week") * weeks
    week_s[...] = r["week"][...] * spread(week_at, 27146)

    if stream:
        for block in range(min(SLOTS, blocks)):
            fetch(jnp.int32(block)).start()
    if first:
        item_at = lax.broadcasted_iota(jnp.int32, (1, items), 1)
        item_at = item_at + lax.axis_index("item") * items
        high, low = split(r["item_t"][...] * spread(item_at, 40503))
        model_w[...] = jnp.concatenate([high, high, low, low], axis=0)
        phi_w[:, : 2 * rank] = jnp.concatenate(
            [high.astype(F32), low.astype(F32)], axis=0
        ).T.astype(BF16)
        phi_w[:, 2 * rank:] = jnp.zeros((items, COLUMNS - 2 * rank), BF16)
        factor_s[...] = r["factor_t"][...].T
        n_item, n_week = (dict(axes)[a] for a in ("item", "week"))
        r["phi_out"][users // 2:, :] = column_sums(r["item_t"][...], r["week"][...], n_item, n_week)
    else:
        summed = r["summed"][...]
        if iteration == 1:
            sums = summed[users // 2:]
            den = sums[:, :rank] * sums[:, rank:]
            r["den_out"][...] = den
            old = r["factor_t"][...].T
        else:
            den = r["den"][...]
            old = r["factor"][...]
        new, sound = update(old, unpack(summed[: users // 2]), den[0:1, :])
        factor_s[...] = new
        r["factor_out"][...] = new
        r["sound_out"][...] = sound if iteration == 1 else sound * r["sound"][...]

    strips = [slice(n * weeks, (n + 1) * weeks) for n in range(tile)]
    chunks = items // COLUMNS
    lhs_s, phi_s = r["lhs_s"], r["phi_s"]

    def operand(user):
        high, low = split(factor_s[pl.ds(user, 1), :] * week_s[...])
        return jnp.concatenate([high, low, high, low], axis=1)

    def push_model(chunk):
        at = pl.ds(chunk % chunks * COLUMNS, COLUMNS)
        pltpu.matmul_push_rhs(model_w[:, at], 0, 0)

    def push_phi(chunk):
        at = pl.ds(chunk % chunks * COLUMNS, COLUMNS)
        pltpu.matmul_push_rhs(phi_w[at, :], 0, 1)

    def matmuls(ahead, total):
        def keep(n, user):
            sums = pltpu.matmul_pop(total[n])
            sums = (sums[:, :rank] + sums[:, rank: 2 * rank]) * week_s[...]
            phi_s[pl.ds(user, 1), :] = jnp.sum(sums, axis=0, keepdims=True)

        push_model(0)
        for n, strip in enumerate(strips):
            lhs_s[strip, :] = operand(n)
            pltpu.matmul_acc_lhs(ahead[n], lhs_s[strip, :], None if n else 0)
        push_model(1)
        push_phi(0)

        def body(block, carry):
            start = block * tile
            before = lax.rem(start + users - tile, users)
            after = jnp.minimum(start + tile, users - tile)
            lagging = []
            if stream:
                fetch(block).wait()

            def add_phi():
                chunk, n, parts = lagging.pop(0)
                if chunk == 0:
                    keep(n, before + n)
                pltpu.matmul_acc_lhs(total[n], parts[0], None if n else 0)
                for part in parts[1:]:
                    pltpu.matmul_acc_lhs(total[n], part)
                if n == 3 * len(strips) // 4:
                    push_phi(chunk + 1)

            for chunk in range(chunks):
                at = slice(chunk * COLUMNS, (chunk + 1) * COLUMNS)
                for n, strip in enumerate(strips):
                    model = pltpu.matmul_pop(ahead[n])
                    if chunk + 1 < chunks:
                        lhs = lhs_s[strip, :]
                    else:
                        lhs = operand(after + n)
                        lhs_s[strip, :] = lhs
                    pltpu.matmul_acc_lhs(ahead[n], lhs, None if n else 0)
                    if n == len(strips) // 4:
                        push_model(chunk + 2)
                    if stream:
                        count = r["slots"][lax.rem(block, SLOTS), n, :, at]
                        count = count.astype(F32)
                        if "small_out" in r:
                            r["small_out"][start + n, :, at] = count.astype(SMALL)
                        count = count.astype(BF16)
                    else:
                        count = counts[start + n, :, at].astype(BF16)
                    inverse = pltpu.reciprocal(model, approx=True, full_range=False)
                    if exact:
                        parts = split(count.astype(F32) * inverse)
                    else:
                        parts = (count * inverse.astype(BF16),)
                    lagging.append((chunk, n, parts))
                    if len(lagging) > LAG:
                        add_phi()
            while lagging:
                add_phi()
            if stream:

                @pl.when(block + SLOTS < blocks)
                def _():
                    fetch(block + SLOTS).start()

            return carry

        lax.fori_loop(0, blocks, body, 0)
        for n in range(tile):
            keep(n, users - tile + n)
        nothing = jnp.zeros((weeks, COLUMNS), BF16)
        for ref in ahead:
            pltpu.matmul_pop(ref)
        for ref in (ahead[0], total[0]):
            pltpu.matmul_acc_lhs(ref, nothing, 0)
            pltpu.matmul_pop(ref)

    pl.run_scoped(matmuls, *[[unit] * tile for unit in units])
    r["phi_out"][: users // 2, :] = pack(phi_s[...])


def last_kernel(factor, summed, den, sound, out, sound_out):
    new, fine = update(factor[...], unpack(summed[...]), den[0:1, :])
    out[...] = new.T
    sound_out[0] = jnp.min(fine * sound[...]).astype(jnp.int32)


def updates(exact, mesh, axes, counts, user_factor, item_factor, week_factor):
    users, rank = user_factor.shape
    weeks, items = counts.shape[1:]
    factor_t, item_t = user_factor.T, item_factor.T
    travel = sorted(axes, reverse=True)

    def shape(dims, dtype=F32):
        return jax.ShapeDtypeStruct(dims, dtype)

    stream = {
        "slots": pltpu.VMEM((SLOTS, FIRST_TILE, weeks, items), jnp.int32),
        "arrived": pltpu.SemaphoreType.DMA((SLOTS,)),
    }
    scratch = {
        "factor_s": pltpu.VMEM((users, rank), F32),
        "week_s": pltpu.VMEM((weeks, rank), F32),
        "phi_s": pltpu.VMEM((users, rank), F32),
        "lhs_s": pltpu.VMEM((NEXT_TILE * weeks, 4 * rank), BF16),
    }
    with jax.sharding.use_abstract_mesh(mesh.abstract_mesh):
        units = [pltpu.ACC(unit)((weeks, COLUMNS), F32) for unit in (0, 1)]

    def sweep(iteration, counts, ins, outs):
        ins = {"counts": counts, "week": week_factor, **ins}
        streamed = counts.dtype == jnp.int32
        scratches = {**stream, **scratch} if streamed else scratch
        names = list(ins) + list(outs) + list(scratches)
        results = pl.pallas_call(
            functools.partial(sweep_kernel, iteration, exact, axes, names, units),
            in_specs=[
                pl.BlockSpec(memory_space=pl.ANY if streamed and n == "counts" else pltpu.VMEM)
                for n in ins
            ],
            out_specs=[pl.BlockSpec(memory_space=pltpu.VMEM)] * len(outs),
            out_shape=list(outs.values()),
            scratch_shapes=list(scratches.values()),
            compiler_params=pltpu.CompilerParams(vmem_limit_bytes=(22 if streamed else 8) * 1024 * 1024),
            cost_estimate=pl.CostEstimate(
                flops=2 * (3 if exact else 2) * users * weeks * items * 256,
                bytes_accessed=4 * users * weeks * items,
                transcendentals=0,
            ),
        )(*ins.values())
        return dict(zip(outs, results))

    packed = shape((users // 2, 2 * rank))
    factor_out, sound_out = shape((users, rank)), shape((8, 128))
    outs = {
        "phi_out": shape((users // 2 + 8, 2 * rank)),
        "model_w": shape((4 * rank, items), BF16),
        "phi_w": shape((items, COLUMNS), BF16),
    }
    if not exact:
        outs["small_out"] = shape(counts.shape, SMALL)
    got = sweep(0, counts, {"factor_t": factor_t, "item_t": item_t}, outs)
    small, weights = got.get("small_out", counts), {n: got[n] for n in ("model_w", "phi_w")}
    summed = sum_over(got["phi_out"], travel)
    got = sweep(
        1, small, {"factor_t": factor_t, "summed": summed, **weights},
        {"phi_out": packed, "factor_out": factor_out, "sound_out": sound_out,
         "den_out": shape((8, rank))},
    )
    den = got["den_out"]
    for iteration in range(2, ITERS):
        got = sweep(
            iteration, small,
            {"factor": got["factor_out"], "summed": sum_over(got["phi_out"], travel),
             "den": den, "sound": got["sound_out"], **weights},
            {"phi_out": packed, "factor_out": factor_out, "sound_out": sound_out},
        )
    out, sound = pl.pallas_call(
        last_kernel,
        in_specs=[pl.BlockSpec(memory_space=pltpu.VMEM)] * 4,
        out_specs=[pl.BlockSpec(memory_space=m) for m in (pltpu.VMEM, pltpu.SMEM)],
        out_shape=[shape((rank, users)), shape((1,), jnp.int32)],
        compiler_params=pltpu.CompilerParams(vmem_limit_bytes=4 * 1024 * 1024),
    )(got["factor_out"], sum_over(got["phi_out"], travel), den, got["sound_out"])
    return out.T, sound.reshape(())


def per_device(mesh, axes, *arrays):
    out, sound = updates(False, mesh, axes, *arrays)
    return lax.cond(sound, lambda *_: out, lambda *a: updates(True, mesh, axes, *a)[0], *arrays)


def solution(mesh):
    axes = tuple(zip(mesh.axis_names, mesh.devices.shape))
    placed = (P(None, "week", "item"), P(), P("item", None), P("week", None))
    run = functools.partial(per_device, mesh, axes)
    return jax.shard_map(run, mesh=mesh, in_specs=placed, out_specs=P(), check_vma=False)
```
